32 devices in a mesh: replica: 8 (over z, x), shard: 4 (over y, core).
Axes of the slice: x: 2, y: 2, z: 4, core: 2. Of those that a mesh axis runs over, the one named last changes fastest.
Arguments:
- tokens: bfloat16 [8, 2, 512, 512], P('replica', None, 'shard'), may hold values from -6 to 6
- cotangent: bfloat16 [8, 2, 512, 512], P('replica', None, 'shard'), may hold values from -6 to 6
- segments: int32 [8, 2, 512], P('replica', None, 'shard'), may hold values from 0 to 2, as said below
- pad_mask: int32 [8, 2, 512], P('replica', None, 'shard'), may hold values from 0 to 1, as said below
- slot_table: int32 [8, 2], P('replica'), may hold values from 0 to 1, as said below
- joined_weight: bfloat16 [512, 1536], P('shard'), may hold values from -0.25 to 0.25
- joined_bias: bfloat16 [1536], P('shard'), may hold values from -2 to 2
- dense_weight: bfloat16 [512, 512], P('shard'), may hold values from -1 to 1
- dense_bias: bfloat16 [512], P('shard'), may hold values from -2 to 2
- expand_weight: bfloat16 [512, 2048], P('shard'), may hold values from -0.25 to 0.25
- expand_bias: bfloat16 [2048], P('shard'), may hold values from -2 to 2
- shrink_weight: bfloat16 [2048, 512], P('shard'), may hold values from -0.125 to 0.125
- shrink_bias: bfloat16 [512], P('shard'), may hold values from -2 to 2
- first_gain: bfloat16 [512], P('shard'), may hold values from 0.5 to 1.5
- first_shift: bfloat16 [512], P('shard'), may hold values from -2 to 2
- second_gain: bfloat16 [512], P('shard'), may hold values from 0.5 to 1.5
- second_shift: bfloat16 [512], P('shard'), may hold values from -2 to 2
Outputs:
- output: bfloat16 [8, 2, 512, 512], P('replica', None, 'shard')
- input_grad: float32 [8, 2, 512, 512], P('replica', None, 'shard')
- grad_joined_weight: float32 [512, 1536], P('shard')
- grad_joined_bias: float32 [1536], P('shard')
- grad_dense_weight: float32 [512, 512], P('shard')
- grad_dense_bias: float32 [512], P('shard')
- grad_expand_weight: float32 [512, 2048], P('shard')
- grad_expand_bias: float32 [2048], P('shard')
- grad_shrink_weight: float32 [2048, 512], P('shard')
- grad_shrink_bias: float32 [512], P('shard')
- grad_first_gain: float32 [512], P('shard')
- grad_first_shift: float32 [512], P('shard')
- grad_second_gain: float32 [512], P('shard')
- grad_second_shift: float32 [512], P('shard')
The draws below stay inside these ranges and needn't reach their ends.
Inputs may be any that keep to these rules, and one draw needn't show every extreme that they name: `slot_table`: every replica has at least one slot that holds a sequence. `pad_mask`: within a slot the real tokens come first; in every replica some slot with a sequence has no padding. `segments`: starts at 0 and never falls along a sequence; in every replica some slot with a sequence has document 0 reaching position 384 or beyond.
All inputs are finite; a program needn't handle non-finite values.
Results may differ from the reference program's by a relative error of at most 0.015.
Values may be sent and summed in bfloat16 or wider, within the bound.
No kernel may reach another device: no remote copies, remote signals or barrier semaphores. Data moves between devices by JAX's collectives and lax.ppermute only.
A program may use at most 320 MiB of HBM per device.

```python
import jax
import jax.numpy as jnp
from jax import lax

D = 512
HEADS = 8
HEAD_DIM = 64
FF = 2048
ROT = 16
PIECE = 128
SLOTS = 2
SEQ_LEN = 512
N_REPLICA = 8


def layout(key):
    slot_index = jnp.arange(SLOTS, dtype=jnp.int32)[None, :]
    reach_slot = jax.random.randint(jax.random.fold_in(key, 11), (N_REPLICA, 1), 0, SLOTS)
    reaching = slot_index == reach_slot
    extra = jax.random.randint(jax.random.fold_in(key, 12), (N_REPLICA, SLOTS), 0, 2)
    live_slots = jnp.where(reaching, 1, extra).astype(jnp.int32)
    cut = jax.random.randint(jax.random.fold_in(key, 13), (N_REPLICA, SLOTS), 0, PIECE)
    lengths = jnp.where(reaching, SEQ_LEN, SEQ_LEN - cut)
    first_lo = jnp.where(reaching, SEQ_LEN - PIECE + 1, 1)
    first_end = jax.random.randint(jax.random.fold_in(key, 14), (N_REPLICA, SLOTS), first_lo, SEQ_LEN + 1)
    second_end = first_end + jax.random.randint(jax.random.fold_in(key, 15), (N_REPLICA, SLOTS), 1, SEQ_LEN)
    places = jnp.arange(SEQ_LEN, dtype=jnp.int32)[None, None, :]
    pads = (places < lengths[:, :, None]).astype(jnp.int32)
    docs = (places >= first_end[:, :, None]).astype(jnp.int32) + (places >= second_end[:, :, None]).astype(jnp.int32)
    return (live_slots, pads, docs)


def draw_slot_table(key, part):
    live_slots, pads, docs = layout(key)
    return live_slots


def draw_pad_mask(key, part):
    live_slots, pads, docs = layout(key)
    return pads


def draw_segments(key, part):
    live_slots, pads, docs = layout(key)
    return docs


def level_of(stream_key, dims, pieces, smallest, top_value):
    level = 1.0
    for dim, parts in pieces:
        draws = jax.random.uniform(jax.random.fold_in(jax.random.fold_in(stream_key, 6), dim), (parts,), jnp.float32, smallest / len(pieces), top_value / len(pieces))
        level = level * jnp.repeat(jnp.exp(draws), dims[dim] // parts).reshape((-1,) + (1,) * (len(dims) - 1 - dim))
    return level


def normal_values(rng, shape, scale, reach, split=(), held_as=jnp.bfloat16):
    level = level_of(rng, shape, split, -0.22, 0.18) if split else 1.0
    values = jax.random.normal(rng, shape, jnp.float32) * scale * level
    return jnp.minimum(jnp.maximum(values, -reach), reach).astype(held_as)


def setup_inputs(seed: int = 0) -> dict:
    arg_keys = jax.random.split(jax.random.key(seed), 18)
    tokens = normal_values(arg_keys[0], (N_REPLICA, SLOTS, SEQ_LEN, D), 1.0, 6.0, ((0, 8), (2, 4)))
    cotangent = normal_values(arg_keys[1], (N_REPLICA, SLOTS, SEQ_LEN, D), 1.0, 6.0, ((0, 8), (2, 4)))
    segments = draw_segments(jax.random.fold_in(arg_keys[17], 71), 0)
    pad_mask = draw_pad_mask(jax.random.fold_in(arg_keys[17], 71), 0)
    slot_table = draw_slot_table(jax.random.fold_in(arg_keys[17], 71), 0)
    joined_weight = normal_values(arg_keys[5], (D, 3 * D), D ** -0.5, 0.25, ((0, 4),))
    joined_bias = normal_values(arg_keys[6], (3 * D,), 0.3, 2.0, ((0, 4),))
    dense_weight = normal_values(arg_keys[7], (D, D), (D // 16) ** -0.5, 1.0, ((0, 4),))
    dense_bias = normal_values(arg_keys[8], (D,), 0.3, 2.0, ((0, 4),))
    expand_weight = normal_values(arg_keys[9], (D, FF), D ** -0.5, 0.25, ((0, 4),))
    expand_bias = normal_values(arg_keys[10], (FF,), 0.3, 2.0, ((0, 4),))
    shrink_weight = normal_values(arg_keys[11], (FF, D), FF ** -0.5, 0.125, ((0, 4),))
    shrink_bias = normal_values(arg_keys[12], (D,), 0.3, 2.0, ((0, 4),))
    first_gain = jnp.clip(1.0 + 0.1 * jax.random.normal(arg_keys[13], (D,), jnp.float32), 0.5, 1.5).astype(jnp.bfloat16)
    first_shift = normal_values(arg_keys[14], (D,), 0.3, 2.0, ((0, 4),))
    second_gain = jnp.clip(1.0 + 0.1 * jax.random.normal(arg_keys[15], (D,), jnp.float32), 0.5, 1.5).astype(jnp.bfloat16)
    second_shift = normal_values(arg_keys[16], (D,), 0.3, 2.0, ((0, 4),))
    return {"tokens": tokens, "cotangent": cotangent, "segments": segments, "pad_mask": pad_mask, "slot_table": slot_table, "joined_weight": joined_weight, "joined_bias": joined_bias, "dense_weight": dense_weight, "dense_bias": dense_bias, "expand_weight": expand_weight, "expand_bias": expand_bias, "shrink_weight": shrink_weight, "shrink_bias": shrink_bias, "first_gain": first_gain, "first_shift": first_shift, "second_gain": second_gain, "second_shift": second_shift}


@jax.custom_vjp
def low(v):
    return lax.optimization_barrier(v.astype(jnp.bfloat16)).astype(jnp.float32)

@jax.custom_vjp
def low_back(v):
    return v

def low_keep(v):
    return (low(v), None)

def low_pass(kept, grad):
    return (grad,)

def back_keep(v):
    return (v, None)

def back_low(kept, grad):
    return (low(grad),)
low.defvjp(low_keep, low_pass)
low_back.defvjp(back_keep, back_low)

def matmul(left, right):
    return jnp.dot(left, right, precision=lax.Precision.HIGHEST, preferred_element_type=jnp.float32)

def layer_norm(values, gain, shift):
    center = values - lax.optimization_barrier(jnp.mean(values, axis=-1, keepdims=True))
    spread = lax.optimization_barrier(jnp.mean(center * center, axis=-1, keepdims=True))
    return center * lax.rsqrt(spread + 1e-05) * gain + shift

def rotate(values, angles):
    half = ROT // 2
    leading = values[..., :half]
    trailing = values[..., half:ROT]
    cosine = jnp.cos(angles)[:, None, :]
    sine = jnp.sin(angles)[:, None, :]
    return jnp.concatenate([leading * cosine - trailing * sine, trailing * cosine + leading * sine, values[..., ROT:]], axis=-1)

def sequence_forward(params, inputs, seg_row, live_row):
    joined_w, joined_b, dense_w, dense_b, expand_w, expand_b, shrink_w, shrink_b, gain_one, shift_one, gain_two, shift_two = params
    first = low(layer_norm(inputs, gain_one, shift_one))
    joined = low_back(matmul(first, joined_w) + joined_b)
    queries = joined[:, :D].reshape(SEQ_LEN, HEADS, HEAD_DIM)
    key_rows = joined[:, D:2 * D].reshape(SEQ_LEN, HEADS, HEAD_DIM)
    value_rows = low(joined[:, 2 * D:].reshape(SEQ_LEN, HEADS, HEAD_DIM))
    places = jnp.arange(SEQ_LEN, dtype=jnp.int32)
    freqs = 10000.0 ** (-2.0 * jnp.arange(ROT // 2, dtype=jnp.float32) / ROT)
    angles = places.astype(jnp.float32)[:, None] * freqs[None, :]
    queries = low(rotate(queries, angles))
    key_rows = low(rotate(key_rows, angles))
    raw = low_back(jnp.einsum('qhd,khd->hqk', queries, key_rows, precision=lax.Precision.HIGHEST))
    scores = raw * (1.0 / HEAD_DIM ** 0.5)
    allowed = (seg_row[:, None] == seg_row[None, :]) & (places[None, :] <= places[:, None]) & (live_row[None, :] > 0) | (places[:, None] == places[None, :])
    scores = jnp.where(allowed[None], scores, -1e+30)
    top = lax.optimization_barrier(jnp.max(scores, axis=-1, keepdims=True))
    expd = jnp.exp(scores - top)
    probs = low(expd / lax.optimization_barrier(jnp.sum(expd, axis=-1, keepdims=True)))
    heads = jnp.einsum('hqk,khd->qhd', probs, value_rows, precision=lax.Precision.HIGHEST).reshape(SEQ_LEN, D)
    heads = low(low_back(heads))
    attention = matmul(heads, dense_w) + dense_b
    second = low(layer_norm(inputs, gain_two, shift_two))
    inner = low_back(matmul(second, expand_w) + expand_b)
    act = low(jax.nn.gelu(inner, approximate=False))
    mlp = matmul(act, shrink_w) + shrink_b
    return inputs + attention + mlp

def reference(tokens, cotangent, segments, pad_mask, slot_table, joined_weight, joined_bias, dense_weight, dense_bias, expand_weight, expand_bias, shrink_weight, shrink_bias, first_gain, first_shift, second_gain, second_shift):
    params = tuple((item.astype(jnp.float32) for item in (joined_weight, joined_bias, dense_weight, dense_bias, expand_weight, expand_bias, shrink_weight, shrink_bias, first_gain, first_shift, second_gain, second_shift)))
    live = (slot_table[:, :, None] * pad_mask).astype(jnp.int32)

    def replica_step(totals, item):
        inputs, cot_rows, seg_rows, live_rows = item
        inputs = inputs.astype(jnp.float32)

        def forward(weights, values):
            return jax.vmap(lambda one_row, seg_one, live_one: sequence_forward(weights, one_row, seg_one, live_one))(values, seg_rows, live_rows)
        result, pullback = jax.vjp(forward, params, inputs)
        weight_grads, input_grads = pullback(cot_rows.astype(jnp.float32) * live_rows.astype(jnp.float32)[..., None])
        totals = jax.tree.map(jnp.add, totals, weight_grads)
        return (totals, (result.astype(jnp.bfloat16), input_grads))
    zeros = tuple((jnp.zeros_like(item) for item in params))
    totals, (output, input_grad) = lax.scan(replica_step, zeros, (tokens, cotangent, segments, live))
    g_joined_w, g_joined_b, g_dense_w, g_dense_b, g_expand_w, g_expand_b, g_shrink_w, g_shrink_b, g_gain_one, g_shift_one, g_gain_two, g_shift_two = totals
    return (output, input_grad, g_joined_w, g_joined_b, g_dense_w, g_dense_b, g_expand_w, g_expand_b, g_shrink_w, g_shrink_b, g_gain_one, g_shift_one, g_gain_two, g_shift_two)
```

```python
import functools

import jax
import jax.numpy as jnp
import numpy as np
from jax import lax
from jax.experimental import pallas as pl
from jax.experimental.pallas import tpu as pltpu
from jax.sharding import PartitionSpec as P

D = 512
HEADS = 8
HEAD_DIM = 64
FF = 2048
ROT = 16
META = 16
VEC = 16

F32 = jnp.float32
BF16 = jnp.bfloat16


def exchange(value, axis, bit):
    size = lax.axis_size(axis)
    return lax.ppermute(value, axis, [(i, i ^ bit) for i in range(size)])


def gathered_by_xor(value, axis):
    size = lax.axis_size(axis)
    held = value[None]
    bits = []
    bit = size // 2
    while bit:
        held = jnp.concatenate([held, exchange(held, axis, bit)], axis=0)
        bits.append(bit)
        bit //= 2
    order = []
    for k in range(size):
        order.append(sum(1 << place for place, b in enumerate(bits) if k & b))
    return held, order


def dot(left, right):
    return jnp.dot(left, right, preferred_element_type=F32)


def dot_tb(left, right):
    return lax.dot_general(left, right, (((1,), (1,)), ((), ())), preferred_element_type=F32)


def dot_ta(left, right):
    return lax.dot_general(left, right, (((0,), (0,)), ((), ())), preferred_element_type=F32)


def normalized(values):
    center = values - jnp.mean(values, axis=-1, keepdims=True)
    spread = jnp.mean(center * center, axis=-1, keepdims=True)
    root = lax.rsqrt(spread + 1e-05)
    return center * root, root


def meta_row(weights, line, start, stop):
    return jnp.concatenate(
        [weights[j, 128 : 128 + META, start:stop].astype(F32)[line : line + 1] for j in range(4)], axis=1
    )


def mlp_kernel(
    place, t0, t1, t2, t3, d0, d1, d2, d3, weights, shrink, bias, mlp_out, e_out, grad_out, vec_out,
    expand_s, second_s, act_s, inner_s, dy_s, *, split,
):
    me = place[0]
    for j in range(4):
        expand_s[j * 128 : (j + 1) * 128, :] = weights[j, 0:128, 384:896]
    gain = meta_row(weights, 1, 256, 384)
    shift = meta_row(weights, 1, 384, 512)
    vec_gain = jnp.zeros((1, D), F32)
    vec_shift = jnp.zeros((1, D), F32)
    vec_bias = jnp.zeros((1, 512), F32)
    vec_dy = jnp.zeros((1, D), F32)
    for k, (tok, cot) in enumerate(((t0, d0), (t1, d1), (t2, d2), (t3, d3))):
        rows = slice(k * 256, (k + 1) * 256)
        hat, _ = normalized(tok[...].astype(F32))
        second = (hat * gain + shift).astype(BF16)
        second_s[rows, :] = second
        inner = dot(second, expand_s[...]) + bias[...]
        half = 0.5 + 0.5 * lax.erf(inner * (0.5**0.5))
        act = (inner * half).astype(BF16)
        act_s[rows, :] = act
        slope = half + inner * jnp.exp(inner * inner * -0.5) * ((0.5 / np.pi) ** 0.5)
        dy = cot[...]
        dy_s[rows, :] = dy
        mlp_out[me ^ k] = dot(act, shrink[...]).reshape(2, 128, D)
        d_inner = (dot_tb(dy, shrink[...]) * slope).astype(BF16)
        inner_s[rows, :] = d_inner
        d_second = dot_tb(d_inner, expand_s[...])
        e_out[me ^ k] = (d_second * gain).reshape(2, 128, D)
        vec_gain += jnp.sum(d_second * hat, axis=0, keepdims=True)
        vec_shift += jnp.sum(d_second, axis=0, keepdims=True)
        vec_bias += jnp.sum(d_inner.astype(F32), axis=0, keepdims=True)
        vec_dy += jnp.sum(dy.astype(F32), axis=0, keepdims=True)
    vec_out[...] = jnp.zeros_like(vec_out)
    vec_out[2:3, :] = vec_gain
    vec_out[3:4, :] = vec_shift
    vec_out[5:6, :] = vec_bias
    vec_out[6:7, :] = vec_dy
    grad_shrink = dot_ta(act_s[...], dy_s[...]).astype(BF16)
    grad_expand = dot_ta(second_s[...], inner_s[...]).astype(BF16)
    if split:
        part = 128 // split
        grad_out[:, 0 : 4 * part, :] = grad_shrink.reshape(split, 4 * part, D)
        for j in range(4):
            grad_out[:, (4 + j) * part : (5 + j) * part, :] = grad_expand[j * 128 : (j + 1) * 128].reshape(
                split, part, D
            )
    else:
        grad_out[0] = grad_shrink
        grad_out[1] = grad_expand


def turned(values, cosine, sine_up, sine_down, sign):
    up = pltpu.roll(values, 120, 1)
    down = pltpu.roll(values, 8, 1)
    return values * cosine + (up * sine_up + down * sine_down) * sign


def attention_kernel(
    place, t0, t1, t2, t3, d0, d1, d2, d3, weights, dense, bias, table, mlp, e_in, vec_in,
    both_out, grad_out, vec_out,
    joined_s, first_s, djoined_s, heads_s, tok_s, dy_s, *, split,
):
    me = place[0]
    for j in range(4):
        joined_s[j * 128 : (j + 1) * 128, :] = weights[j, 0:128, 0:384]
    for k, (tok, cot) in enumerate(((t0, d0), (t1, d1), (t2, d2), (t3, d3))):
        for s in range(2):
            start = pl.multiple_of(s * 512 + (me ^ k) * 128, 128)
            tok_s[pl.ds(start, 128), :] = tok[s * 128 : (s + 1) * 128, :]
            dy_s[pl.ds(start, 128), :] = cot[s * 128 : (s + 1) * 128, :]
    gain = meta_row(weights, 1, 0, 128)
    shift = meta_row(weights, 1, 128, 256)
    low_half = lax.broadcasted_iota(jnp.int32, (1, 128), 1) < HEAD_DIM
    joined_bias = jnp.concatenate(
        [bias[0:1, 0:384]], axis=1
    )
    vec_gain = jnp.zeros((1, D), F32)
    vec_shift = jnp.zeros((1, D), F32)
    vec_bias = jnp.zeros((1, 384), F32)
    cosine = table[:, 0:128]
    sine_up = table[:, 128:256]
    sine_down = table[:, 256:384]
    zero = jnp.zeros((), BF16)
    for s in range(2):
        rows = slice(s * 512, (s + 1) * 512)
        hat, _ = normalized(tok_s[rows, :].astype(F32))
        first = (hat * gain + shift).astype(BF16)
        first_s[rows, :] = first
        joined = dot(first, joined_s[...]) + joined_bias
        query = (turned(joined[:, 0:128], cosine, sine_up, sine_down, 1.0) * (HEAD_DIM**-0.5)).astype(BF16)
        key = turned(joined[:, 128:256], cosine, sine_up, sine_down, 1.0).astype(BF16)
        value = joined[:, 256:384].astype(BF16)
        dy = dy_s[rows, :]
        d_heads = dot_tb(dy, dense[...]).astype(BF16)
        query_doc = jnp.transpose(
            jnp.broadcast_to(meta_row(weights, 0, s * 128, (s + 1) * 128), (8, 512))
        )[:, 0:1]
        key_doc = meta_row(weights, 0, 256 + s * 128, 256 + (s + 1) * 128)
        query_grads = []
        heads_parts = []
        key_grad = jnp.zeros((128, 512), F32)
        value_grad = jnp.zeros((128, 512), F32)
        for block in range(2):
            lo, hi = block * 256, (block + 1) * 256
            at = lax.broadcasted_iota(jnp.int32, (256, hi), 0) + lo
            to = lax.broadcasted_iota(jnp.int32, (256, hi), 1)
            allowed = ((query_doc[lo:hi] == key_doc[:, :hi]) & (to <= at)) | (to == at)
            out = jnp.zeros((256, 128), F32)
            query_grad = jnp.zeros((256, 128), F32)
            key_part = jnp.zeros((128, hi), F32)
            value_part = jnp.zeros((128, hi), F32)
            for h in range(2):
                mine = low_half if h == 0 else jnp.logical_not(low_half)
                q_h = jnp.where(mine, query[lo:hi], zero)
                k_h = jnp.where(mine, key[:hi], zero)
                v_h = jnp.where(mine, value[:hi], zero)
                g_h = jnp.where(mine, d_heads[lo:hi], zero)
                scores = jnp.where(allowed, dot_tb(q_h, k_h), -1e30)
                top = jnp.max(scores, axis=-1, keepdims=True)
                expd = jnp.exp(scores - top)
                probs = expd * (1.0 / jnp.sum(expd, axis=-1, keepdims=True))
                probs_low = probs.astype(BF16)
                out += dot(probs_low, v_h)
                d_probs = dot_tb(g_h, v_h)
                weighted = d_probs * probs
                d_scores = (weighted - probs * jnp.sum(weighted, axis=-1, keepdims=True)).astype(BF16)
                query_grad += dot(d_scores, k_h)
                key_part += dot_ta(q_h, d_scores)
                value_part += dot_ta(g_h, probs_low)
            query_grads.append(query_grad)
            heads_parts.append(out)
            if hi < 512:
                pad = jnp.zeros((128, 512 - hi), F32)
                key_part = jnp.concatenate([key_part, pad], axis=1)
                value_part = jnp.concatenate([value_part, pad], axis=1)
            key_grad += key_part
            value_grad += value_part
        heads = jnp.concatenate(heads_parts, axis=0).astype(BF16)
        heads_s[rows, :] = heads
        query_grad = jnp.concatenate(query_grads, axis=0) * (HEAD_DIM**-0.5)
        d_joined = jnp.concatenate(
            [
                turned(query_grad, cosine, sine_up, sine_down, -1.0),
                turned(jnp.transpose(key_grad), cosine, sine_up, sine_down, -1.0),
                jnp.transpose(value_grad),
            ],
            axis=1,
        ).astype(BF16)
        djoined_s[rows, :] = d_joined
        vec_bias += jnp.sum(d_joined.astype(F32), axis=0, keepdims=True)
        d_first = dot_tb(d_joined, joined_s[...])
        vec_gain += jnp.sum(d_first * hat, axis=0, keepdims=True)
        vec_shift += jnp.sum(d_first, axis=0, keepdims=True)
        grad_in = d_first * gain
        attention = dot(heads, dense[...]) + bias[1:2, :]
        for j in range(4):
            piece = slice(j * 128, (j + 1) * 128)
            both_out[j, 0, s] = (attention[piece] + mlp[j, s]).astype(BF16)
            both_out[j, 1, s] = (grad_in[piece] + e_in[j, s]).astype(BF16)
    vec_out[...] = vec_in[...]
    vec_out[0:1, :] = vec_gain
    vec_out[1:2, :] = vec_shift
    vec_out[4:5, 0:384] = vec_bias
    grad_joined = dot_ta(first_s[...], djoined_s[...]).astype(BF16)
    grad_dense = dot_ta(heads_s[...], dy_s[...]).astype(BF16)
    if split:
        part = 128 // split
        for j in range(4):
            grad_out[:, j * part : (j + 1) * part, 0:384] = grad_joined[j * 128 : (j + 1) * 128].reshape(
                split, part, 384
            )
            grad_out[:, j * part : (j + 1) * part, 384:512] = grad_dense[:, j * 128 : (j + 1) * 128].reshape(
                split, part, 128
            )
    else:
        for j in range(4):
            grad_out[j, :, 0:384] = grad_joined[j * 128 : (j + 1) * 128]
            grad_out[j, :, 384:512] = grad_dense[:, j * 128 : (j + 1) * 128]


def finish_kernel(arrived, tok, cot, out, grad):
    for s in range(2):
        tokens = tok[s].astype(F32)
        total = tokens
        e = jnp.zeros((128, D), F32)
        for j in range(4):
            total = total + arrived[j, 0, s].astype(F32)
            e = e + arrived[j, 1, s].astype(F32)
        out[s] = total.astype(BF16)
        hat, root = normalized(tokens)
        mean_e = jnp.mean(e, axis=-1, keepdims=True)
        mean_eh = jnp.mean(e * hat, axis=-1, keepdims=True)
        grad[s] = cot[s].astype(F32) + root * (e - mean_e - hat * mean_eh)


def rope_table(length):
    half = ROT // 2
    freqs = (10000.0 ** (-2.0 * np.arange(half, dtype=np.float64) / ROT)).astype(np.float32)
    angles = np.arange(length, dtype=np.float32)[:, None] * freqs[None, :]
    cosine = np.ones((length, HEAD_DIM), np.float32)
    up = np.zeros((length, HEAD_DIM), np.float32)
    down = np.zeros((length, HEAD_DIM), np.float32)
    cosine[:, :half] = np.cos(angles)
    cosine[:, half:ROT] = np.cos(angles)
    up[:, :half] = -np.sin(angles)
    down[:, half:ROT] = np.sin(angles)
    return np.concatenate([np.tile(part, (1, 2)) for part in (cosine, up, down)], axis=1)


def per_device(
    tokens,
    cotangent,
    segments,
    pad_mask,
    slot_table,
    joined_weight,
    joined_bias,
    dense_weight,
    dense_bias,
    expand_weight,
    expand_bias,
    shrink_weight,
    shrink_bias,
    first_gain,
    first_shift,
    second_gain,
    second_shift,
):
    replicas = lax.axis_size("replica")
    me = lax.axis_index("shard")
    mine = lax.axis_index("replica")
    place = me.astype(jnp.int32).reshape(1)
    split = replicas if (128 // replicas) % 16 == 0 else 0
    part = 128 // replicas
    params = pltpu.CompilerParams(vmem_limit_bytes=56 * 1024 * 1024)
    smem = pl.BlockSpec(memory_space=pltpu.SMEM)
    vmem = pl.BlockSpec(memory_space=pltpu.VMEM)

    tok = tokens[0]
    live = slot_table[0][:, None] * pad_mask[0]
    seg = segments[0]
    dy = jnp.where(live[:, :, None] > 0, cotangent[0], jnp.zeros((), BF16))

    def everyone(own):
        across = exchange(own, "shard", 2)
        near = exchange(own, "shard", 1)
        far = exchange(across, "shard", 1)
        return [item.reshape(256, D) for item in (own, near, across, far)]

    code = jnp.where(live > 0, seg, -1)
    line0 = jnp.concatenate(
        [seg.reshape(256).astype(BF16), code.reshape(256).astype(BF16), joined_bias]
    )
    line1 = jnp.concatenate(
        [first_gain, first_shift, second_gain, second_shift, jnp.zeros((384,), BF16)]
    )
    meta = jnp.concatenate([line0[None], line1[None], jnp.zeros((META - 2, 896), BF16)], axis=0)
    packed = jnp.concatenate(
        [
            joined_weight.reshape(128, 3, 4, 128).transpose(2, 0, 1, 3).reshape(4, 128, 384),
            expand_weight.reshape(128, 4, 512).transpose(1, 0, 2),
        ],
        axis=2,
    )
    packed = jnp.concatenate([packed, jnp.broadcast_to(meta[None], (4, META, 896))], axis=1)
    toks = everyone(tok)
    weights = lax.all_to_all(packed, "shard", 0, 0, tiled=True)
    dys = everyone(dy)

    rows1024 = jax.ShapeDtypeStruct((4, 2, 128, D), F32)
    mlp_grad_shape = (replicas, 8 * part, D) if split else (2, 512, D)
    mlp, e_second, mlp_grad, vec_mlp = pl.pallas_call(
        functools.partial(mlp_kernel, split=split),
        out_shape=(rows1024, rows1024, jax.ShapeDtypeStruct(mlp_grad_shape, BF16), jax.ShapeDtypeStruct((8, D), F32)),
        in_specs=[smem] + [vmem] * 11,
        out_specs=(vmem,) * 4,
        scratch_shapes=[
            pltpu.VMEM((512, 512), BF16),
            pltpu.VMEM((1024, D), BF16),
            pltpu.VMEM((1024, 512), BF16),
            pltpu.VMEM((1024, 512), BF16),
            pltpu.VMEM((1024, D), BF16),
        ],
        compiler_params=params,
        name="mlp_branch",
    )(place, *toks, *dys, weights, shrink_weight, expand_bias.astype(F32).reshape(1, 512))

    def chunks_of(pair):
        shrink_part = pair[0].reshape(replicas, 4 * part, D)
        expand_part = pair[1].reshape(4, replicas, part, D).transpose(1, 0, 2, 3).reshape(replicas, 4 * part, D)
        return jnp.concatenate([shrink_part, expand_part], axis=1)

    if not split:
        mlp_grad = chunks_of(mlp_grad)

    def summed(chunks):
        return jnp.sum(lax.all_to_all(chunks, "replica", 0, 0, tiled=True).astype(F32), axis=0)

    mlp_own = summed(mlp_grad).astype(BF16)
    expand_own = lax.all_to_all(mlp_own[4 * part :].reshape(4, part, D), "shard", 0, 0, tiled=True)
    mlp_all, order = gathered_by_xor(
        jnp.concatenate([mlp_own[: 4 * part], expand_own.reshape(4 * part, D)], axis=0), "replica"
    )

    bias_full = weights[:, 128, 512:896].reshape(3 * D)
    bias_mine = lax.dynamic_slice_in_dim(bias_full.reshape(3, 4, 128), me, 1, axis=1).reshape(1, 384).astype(F32)
    row_bias = (dense_bias.astype(F32) + shrink_bias.astype(F32)).reshape(1, 128)
    row_bias = jnp.where(
        (jnp.arange(4, dtype=jnp.int32) == me)[:, None], row_bias, 0.0
    ).reshape(1, D)
    bias = jnp.concatenate([jnp.pad(bias_mine, ((0, 0), (0, 128))), row_bias], axis=0)
    att_grad_shape = (replicas, 4 * part, D) if split else (4, 128, D)
    both, att_grad, vec = pl.pallas_call(
        functools.partial(attention_kernel, split=split),
        out_shape=(
            jax.ShapeDtypeStruct((4, 2, 2, 128, D), BF16),
            jax.ShapeDtypeStruct(att_grad_shape, BF16),
            jax.ShapeDtypeStruct((8, D), F32),
        ),
        in_specs=[smem] + [vmem] * 15,
        out_specs=(vmem,) * 3,
        scratch_shapes=[
            pltpu.VMEM((512, 384), BF16),
            pltpu.VMEM((1024, D), BF16),
            pltpu.VMEM((1024, 384), BF16),
            pltpu.VMEM((1024, 128), BF16),
            pltpu.VMEM((1024, D), BF16),
            pltpu.VMEM((1024, D), BF16),
        ],
        compiler_params=params,
        name="attention_branch",
    )(place, *toks, *dys, weights, dense_weight, bias, rope_table(512), mlp, e_second, vec_mlp)
    if not split:
        att_grad = att_grad.reshape(4, replicas, part, D).transpose(1, 0, 2, 3).reshape(replicas, 4 * part, D)

    def two_lines(values):
        high = values.astype(BF16)
        left = (values - high.astype(F32)).astype(BF16)
        return high, left

    high, left = two_lines(vec)
    lines = jnp.stack([high, left], axis=1)
    lines = jnp.pad(lines, ((0, replicas - 8), (0, VEC - 2), (0, 0)))
    att_sum = summed(jnp.concatenate([att_grad, lines], axis=1))
    vec_high, vec_left = two_lines(att_sum[4 * part] + att_sum[4 * part + 1])
    att_own = att_sum[: 4 * part].astype(BF16).reshape(4, part, D)
    line_own = jnp.pad(jnp.stack([vec_high, vec_left]), ((0, VEC - 2), (0, 0)))
    shared = lax.all_to_all(
        jnp.concatenate([att_own, jnp.broadcast_to(line_own[None], (4, VEC, D))], axis=1),
        "shard", 0, 0, tiled=True,
    )
    att_mixed = jnp.concatenate([shared[:, :part, :384], att_own[:, :, 384:]], axis=2)
    att_all, order = gathered_by_xor(
        jnp.concatenate([att_mixed.reshape(4 * part, D), shared[:, part : part + 2].reshape(8, D)], axis=0),
        "replica",
    )

    arrived = lax.all_to_all(both, "shard", 0, 0, tiled=True)
    output, input_grad = pl.pallas_call(
        finish_kernel,
        out_shape=(jax.ShapeDtypeStruct((2, 128, D), BF16), jax.ShapeDtypeStruct((2, 128, D), F32)),
        in_specs=[vmem] * 3,
        out_specs=(vmem,) * 2,
        compiler_params=params,
        name="finish_rows",
    )(arrived, tok, dy)

    def in_order(held):
        places = jnp.asarray(order, jnp.int32)[mine ^ jnp.arange(replicas, dtype=jnp.int32)]
        return held[places]

    mlp_done = in_order(mlp_all).astype(F32)
    att_done = in_order(att_all).astype(F32)
    grad_shrink = mlp_done[:, : 4 * part].reshape(512, D)
    grad_expand = (
        mlp_done[:, 4 * part :].reshape(replicas, 4, part, 512).transpose(0, 2, 1, 3).reshape(128, FF)
    )
    mats = att_done[:, : 4 * part].reshape(replicas, 4, part, 512)
    grad_joined = mats[..., :384].reshape(replicas, 4, part, 3, 128).transpose(0, 2, 3, 1, 4).reshape(128, 3 * D)
    grad_dense = mats[..., 384:].transpose(0, 2, 1, 3).reshape(128, D)
    vecs = att_done[:8, 4 * part :].reshape(8, 4, 2, D).sum(axis=2)
    gains = lax.dynamic_slice_in_dim(vecs[:4].sum(axis=1), me * 128, 128, axis=1)
    joined_line = vecs[4, :, :384].reshape(4, 3, 128).transpose(1, 0, 2).reshape(3 * D)
    own = lax.dynamic_index_in_dim(vecs[5:7], me, axis=1, keepdims=False)
    dense_line = lax.dynamic_slice_in_dim(own[1], me * 128, 128, axis=0)
    return (
        output[None],
        input_grad[None],
        grad_joined,
        lax.dynamic_slice_in_dim(joined_line, me * 384, 384, axis=0),
        grad_dense,
        dense_line,
        grad_expand,
        own[0],
        grad_shrink,
        dense_line,
        gains[0],
        gains[1],
        gains[2],
        gains[3],
    )


def solution(mesh):
    rows = P("replica", None, "shard", None)
    codes = P("replica", None, "shard")
    matrix = P("shard", None)
    vector = P("shard")
    return jax.shard_map(
        per_device,
        mesh=mesh,
        in_specs=(rows, rows, codes, codes, P("replica", None))
        + (matrix, vector) * 4
        + (vector,) * 4,
        out_specs=(rows, rows) + (matrix, vector) * 4 + (vector,) * 4,
        check_vma=False,
    )
```

```python
import functools

import jax
import jax.numpy as jnp
import numpy as np
from jax import lax
from jax.experimental import pallas as pl
from jax.experimental.pallas import tpu as pltpu
from jax.sharding import PartitionSpec as P

D = 512
HEADS = 8
HEAD_DIM = 64
FF = 2048
ROT = 16
META = 16

F32 = jnp.float32
BF16 = jnp.bfloat16


def exchange(value, axis, bit):
    size = lax.axis_size(axis)
    return lax.ppermute(value, axis, [(i, i ^ bit) for i in range(size)])


def xor_order(bits):
    found = [0]
    for bit in reversed(bits):
        found = found + [number | bit for number in found]
    return found


def stages_of(size):
    bits = [1 << place for place in range(size.bit_length() - 1)]
    return bits, bits[1::-1] + bits[2:]


def joint_exchange(one, other, axis, bit_one, bit_other):
    if bit_one != bit_other:
        return exchange(one, axis, bit_one), exchange(other, axis, bit_other)
    cut = one.shape[1]
    arrived = exchange(jnp.concatenate([one, other], axis=1), axis, bit_one)
    return arrived[:, :cut], arrived[:, cut:]


def scatter_sum(keeps, sends, axis):
    for bits in zip(*stages_of(lax.axis_size(axis)), strict=True):
        arrived = joint_exchange(*sends, axis, *bits)
        totals = [keep.astype(F32) + new.astype(F32) for keep, new in zip(keeps, arrived, strict=True)]
        half = totals[0].shape[0] // 2
        if half:
            sends = [total[half:].astype(BF16) for total in totals]
            keeps = [total[:half] for total in totals]
    return [total[0].astype(BF16) for total in totals]


def gather_back(one, other, axis):
    held = [one[None], other[None]]
    stages = list(zip(*stages_of(lax.axis_size(axis)), strict=True))[::-1]
    for number, bits in enumerate(stages):
        arrived = joint_exchange(*held, axis, *bits)
        if number == len(stages) - 1:
            return [(mine, new) for mine, new in zip(held, arrived, strict=True)]
        held = [jnp.concatenate([mine, new], axis=0) for mine, new in zip(held, arrived, strict=True)]


def dot(left, right):
    return jnp.dot(left, right, preferred_element_type=F32)


def dot_tb(left, right):
    return lax.dot_general(left, right, (((1,), (1,)), ((), ())), preferred_element_type=F32)


def dot_ta(left, right):
    return lax.dot_general(left, right, (((0,), (0,)), ((), ())), preferred_element_type=F32)


def normalized(values):
    center = values - jnp.mean(values, axis=-1, keepdims=True)
    spread = jnp.mean(center * center, axis=-1, keepdims=True)
    root = lax.rsqrt(spread + 1e-05)
    return center * root, root


def pack_kernel(place, joined, expand, meta, own, near, across):
    me, column = place[0], place[1] % 2

    def joined_block(target, j):
        for part in range(3):
            start = pl.multiple_of(part * D + j * 128, 128)
            target[0:128, part * 128 : (part + 1) * 128] = joined[:, pl.ds(start, 128)]
        target[0:128, 384:512] = jnp.zeros((128, 128), BF16)
        target[128:, :] = meta[...]

    def expand_block(target, j):
        target[0:128, :] = expand[:, pl.ds(pl.multiple_of(j * 512, 512), 512)]
        target[128:, :] = meta[...]

    expand_block(own.at[0], me)
    joined_block(own.at[1], me)
    expand_block(near.at[0], me ^ 1)
    joined_block(near.at[1], me ^ 1)

    @pl.when(column == 0)
    def _():
        expand_block(across.at[0], me ^ 2)
        expand_block(across.at[1], me ^ 3)

    @pl.when(column == 1)
    def _():
        joined_block(across.at[0], me ^ 2)
        joined_block(across.at[1], me ^ 3)


def unpack(place, blocks, kind, weight_s, meta_s):
    own, near, across, beside, far = blocks
    me, column = place[0], place[1] % 2
    width = weight_s.shape[1]

    def put(k, block):
        weight_s[pl.ds(pl.multiple_of((me ^ k) * 128, 128), 128), :] = block[0:128, 0:width]

    put(0, own[kind])
    put(1, near[kind])

    @pl.when(column == kind)
    def _():
        put(2, across[0])
        put(3, far[0])

    @pl.when(column != kind)
    def _():
        put(2, beside[0])
        put(3, far[1])

    for k, block in enumerate((own[0], near[0], across[0], far[0])):
        meta_s[me ^ k] = block[128:, :].astype(F32)


def meta_row(meta_s, line, start, stop):
    return jnp.concatenate([meta_s[j, line : line + 1, start:stop] for j in range(4)], axis=1)


def mlp_kernel(
    place, t0, t1, t2, t3, d0, d1, d2, d3, w0, w1, w2, w3, w4, shrink, bias, mlp_out, e_out, vec_out, *rest, split
):
    outs, (expand_s, meta_s, second_s, act_s, inner_s, dy_s, shrink_s, grad_s) = rest[:-8], rest[-8:]
    me, mine = place[0], place[1]
    unpack(place, (w0, w1, w2, w3, w4), 0, expand_s, meta_s)
    gain = meta_row(meta_s, 1, 256, 384)
    shift = meta_row(meta_s, 1, 384, 512)
    vec_gain = jnp.zeros((1, D), F32)
    vec_shift = jnp.zeros((1, D), F32)
    vec_bias = jnp.zeros((1, 512), F32)
    vec_dy = jnp.zeros((1, D), F32)
    for k, (tok, cot) in enumerate(((t0, d0), (t1, d1), (t2, d2), (t3, d3))):
        rows = slice(k * 256, (k + 1) * 256)
        hat, _ = normalized(tok[...].astype(F32))
        second = (hat * gain + shift).astype(BF16)
        second_s[rows, :] = second
        inner = dot(second, expand_s[...]) + bias[...]
        half = 0.5 + 0.5 * lax.erf(inner * (0.5**0.5))
        act = (inner * half).astype(BF16)
        act_s[rows, :] = act
        slope = half + inner * jnp.exp(inner * inner * -0.5) * ((0.5 / np.pi) ** 0.5)
        dy = cot[...]
        dy_s[rows, :] = dy
        mlp_out[me ^ k] = dot(act, shrink[...]).reshape(2, 128, D)
        d_inner = (dot_tb(dy, shrink[...]) * slope).astype(BF16)
        inner_s[rows, :] = d_inner
        d_second = dot_tb(d_inner, expand_s[...])
        e_out[me ^ k] = (d_second * gain).reshape(2, 128, D)
        vec_gain += jnp.sum(d_second * hat, axis=0, keepdims=True)
        vec_shift += jnp.sum(d_second, axis=0, keepdims=True)
        vec_bias += jnp.sum(d_inner.astype(F32), axis=0, keepdims=True)
        vec_dy += jnp.sum(dy.astype(F32), axis=0, keepdims=True)
    vec_out[...] = jnp.zeros_like(vec_out)
    vec_out[2:3, :] = vec_gain
    vec_out[3:4, :] = vec_shift
    vec_out[5:6, :] = vec_bias
    vec_out[6:7, :] = vec_dy
    grad_shrink = dot_ta(act_s[...], dy_s[...]).astype(BF16)
    grad_expand = dot_ta(second_s[...], inner_s[...]).astype(BF16)
    if not split:
        outs[0][0] = grad_shrink
        outs[0][1] = grad_expand
        return
    part = 128 // split
    shrink_s[...] = grad_shrink.reshape(split, 4 * part, D)
    for j in range(4):
        grad_s[:, me ^ j] = grad_expand[j * 128 : (j + 1) * 128].reshape(split, part, D)
    orders = [xor_order(bits[1:]) for bits in stages_of(split)]
    firsts = [bits[0] for bits in stages_of(split)]
    for i, c in enumerate(orders[0]):
        outs[0][i] = shrink_s[mine ^ c]
        outs[1][i] = shrink_s[mine ^ c ^ firsts[0]]
    for i, c in enumerate(orders[1]):
        outs[2][i] = grad_s[mine ^ c].reshape(4 * part, D)
        outs[3][i] = grad_s[mine ^ c ^ firsts[1]].reshape(4 * part, D)


def turned(values, cosine, sine_up, sine_down, sign):
    up = pltpu.roll(values, 120, 1)
    down = pltpu.roll(values, 8, 1)
    return values * cosine + (up * sine_up + down * sine_down) * sign


def attention_kernel(
    place, t0, t1, t2, t3, d0, d1, d2, d3, w0, w1, w2, w3, w4, dense, out_bias, table, mlp, e_in, vec_in, *rest,
    slot, split,
):
    s = slot
    if s == 0:
        (keep_out, send_out, joined_out, dense_out, vec_out), rest = rest[:5], rest[5:]
    else:
        (joined_in, dense_in), rest = rest[:2], rest[2:]
        (keep_out, send_out), rest = rest[:2], rest[2:]
    outs, (joined_s, meta_s, bias_s, tok_s, dy_s, both_s, grad_s) = rest[:-7], rest[-7:]
    me, mine = place[0], place[1]
    unpack(place, (w0, w1, w2, w3, w4), 1, joined_s, meta_s)
    for k, (tok, cot) in enumerate(((t0, d0), (t1, d1), (t2, d2), (t3, d3))):
        start = pl.multiple_of((me ^ k) * 128, 128)
        tok_s[pl.ds(start, 128), :] = tok[s * 128 : (s + 1) * 128, :]
        dy_s[pl.ds(start, 128), :] = cot[s * 128 : (s + 1) * 128, :]
    gain = meta_row(meta_s, 1, 0, 128)
    shift = meta_row(meta_s, 1, 128, 256)
    bias_s[0:1, :] = meta_row(meta_s, 2, 0, 384)
    joined_bias = jnp.concatenate(
        [bias_s[0:1, pl.ds(pl.multiple_of(part * D + me * 128, 128), 128)] for part in range(3)], axis=1
    )
    low_half = lax.broadcasted_iota(jnp.int32, (1, 128), 1) < HEAD_DIM
    cosine = table[:, 0:128]
    sine_up = table[:, 128:256]
    sine_down = table[:, 256:384]
    zero = jnp.zeros((), BF16)
    hat, _ = normalized(tok_s[...].astype(F32))
    first = (hat * gain + shift).astype(BF16)
    joined = dot(first, joined_s[...]) + joined_bias
    query = (turned(joined[:, 0:128], cosine, sine_up, sine_down, 1.0) * (HEAD_DIM**-0.5)).astype(BF16)
    key = turned(joined[:, 128:256], cosine, sine_up, sine_down, 1.0).astype(BF16)
    value = joined[:, 256:384].astype(BF16)
    dy = dy_s[...]
    d_heads = dot_tb(dy, dense[...]).astype(BF16)
    query_doc = jnp.transpose(
        jnp.broadcast_to(meta_row(meta_s, 0, s * 128, (s + 1) * 128), (8, 512))
    )[:, 0:1]
    key_doc = meta_row(meta_s, 0, 256 + s * 128, 256 + (s + 1) * 128)
    query_grads = []
    heads_parts = []
    key_grad = jnp.zeros((128, 512), F32)
    value_grad = jnp.zeros((128, 512), F32)
    for block in range(2):
        lo, hi = block * 256, (block + 1) * 256
        at = lax.broadcasted_iota(jnp.int32, (256, hi), 0) + lo
        to = lax.broadcasted_iota(jnp.int32, (256, hi), 1)
        allowed = ((query_doc[lo:hi] == key_doc[:, :hi]) & (to <= at)) | (to == at)
        out = jnp.zeros((256, 128), F32)
        query_grad = jnp.zeros((256, 128), F32)
        key_part = jnp.zeros((128, hi), F32)
        value_part = jnp.zeros((128, hi), F32)
        for h in range(2):
            ours = low_half if h == 0 else jnp.logical_not(low_half)
            q_h = jnp.where(ours, query[lo:hi], zero)
            k_h = jnp.where(ours, key[:hi], zero)
            v_h = jnp.where(ours, value[:hi], zero)
            g_h = jnp.where(ours, d_heads[lo:hi], zero)
            scores = jnp.where(allowed, dot_tb(q_h, k_h), -1e30)
            top = jnp.max(scores, axis=-1, keepdims=True)
            expd = jnp.exp(scores - top)
            probs = expd * (1.0 / jnp.sum(expd, axis=-1, keepdims=True))
            probs_low = probs.astype(BF16)
            out += dot(probs_low, v_h)
            d_probs = dot_tb(g_h, v_h)
            weighted = d_probs * probs
            d_scores = (weighted - probs * jnp.sum(weighted, axis=-1, keepdims=True)).astype(BF16)
            query_grad += dot(d_scores, k_h)
            key_part += dot_ta(q_h, d_scores)
            value_part += dot_ta(g_h, probs_low)
        query_grads.append(query_grad)
        heads_parts.append(out)
        if hi < 512:
            pad = jnp.zeros((128, 512 - hi), F32)
            key_part = jnp.concatenate([key_part, pad], axis=1)
            value_part = jnp.concatenate([value_part, pad], axis=1)
        key_grad += key_part
        value_grad += value_part
    heads = jnp.concatenate(heads_parts, axis=0).astype(BF16)
    query_grad = jnp.concatenate(query_grads, axis=0) * (HEAD_DIM**-0.5)
    d_joined = jnp.concatenate(
        [
            turned(query_grad, cosine, sine_up, sine_down, -1.0),
            turned(jnp.transpose(key_grad), cosine, sine_up, sine_down, -1.0),
            jnp.transpose(value_grad),
        ],
        axis=1,
    ).astype(BF16)
    d_first = dot_tb(d_joined, joined_s[...])
    grad_in = d_first * gain
    own_columns = lax.broadcasted_iota(jnp.int32, (1, D), 1) // 128 == me
    attention = dot(heads, dense[...]) + jnp.where(own_columns, jnp.concatenate([out_bias[...]] * 4, axis=1), 0.0)
    for j in range(4):
        piece = slice(j * 128, (j + 1) * 128)
        both_s[j, 0] = (attention[piece] + mlp[j, s]).astype(BF16)
        both_s[j, 1] = (grad_in[piece] + e_in[j, s]).astype(BF16)
    for i in range(2):
        keep_out[i] = both_s[me ^ (2 * i)]
        send_out[i] = both_s[me ^ (2 * i + 1)]
    grad_joined = dot_ta(first, d_joined)
    grad_dense = dot_ta(heads, dy)
    vec = vec_in[...]
    line = lax.broadcasted_iota(jnp.int32, (8, D), 0)
    vec = vec + jnp.where(line == 0, jnp.sum(d_first * hat, axis=0, keepdims=True), 0.0)
    vec = vec + jnp.where(line == 1, jnp.sum(d_first, axis=0, keepdims=True), 0.0)
    bias_line = jnp.concatenate(
        [jnp.sum(d_joined.astype(F32), axis=0, keepdims=True), jnp.zeros((1, 128), F32)], axis=1
    )
    vec = vec + jnp.where(line == 4, bias_line, 0.0)
    if s == 0:
        joined_out[...] = grad_joined
        dense_out[...] = grad_dense
        vec_out[...] = vec
        return
    grad_joined = (grad_joined + joined_in[...]).astype(BF16)
    grad_dense = (grad_dense + dense_in[...]).astype(BF16)
    if not split:
        for j in range(4):
            outs[0][j, :, 0:384] = grad_joined[j * 128 : (j + 1) * 128]
            outs[0][j, :, 384:512] = grad_dense[:, j * 128 : (j + 1) * 128]
        outs[1][...] = vec
        return
    part = 128 // split
    for j in range(4):
        grad_s[:, me ^ j, :, 0:384] = grad_joined[j * 128 : (j + 1) * 128].reshape(split, part, 384)
        grad_s[:, j, :, 384:512] = grad_dense[:, j * 128 : (j + 1) * 128].reshape(split, part, 128)
    for r in range(split):
        grad_s[r, 4] = jnp.broadcast_to(vec[r % 8 : r % 8 + 1], (part, D)).astype(BF16)
    orders = [xor_order(bits[1:]) for bits in stages_of(split)]
    firsts = [bits[0] for bits in stages_of(split)]
    for number, (target, bit) in enumerate(((0, 0), (1, firsts[0]))):
        for i, c in enumerate(orders[0]):
            block = grad_s[mine ^ c ^ bit]
            outs[target][i, 0 : 2 * part] = block[0:2].reshape(2 * part, D)
            outs[target][i, 2 * part : 3 * part] = block[4]
    for target, bit in ((2, 0), (3, firsts[1])):
        for i, c in enumerate(orders[1]):
            outs[target][i] = grad_s[mine ^ c ^ bit][2:4].reshape(2 * part, D)


def finish_kernel(keep, arrived, tok, cot, out, grad):
    tokens = tok[...].astype(F32)
    total = tokens + keep[0] + arrived[0].astype(F32)
    e = keep[1] + arrived[1].astype(F32)
    out[...] = total.astype(BF16)
    hat, root = normalized(tokens)
    mean_e = jnp.mean(e, axis=-1, keepdims=True)
    mean_eh = jnp.mean(e * hat, axis=-1, keepdims=True)
    grad[...] = cot[...].astype(F32) + root * (e - mean_e - hat * mean_eh)


def mlp_place_kernel(place, a0, a1, b0, b1, shrink_out, expand_out, *, split):
    me, mine = place[0], place[1]
    part = 128 // split
    orders = [xor_order(bits) for bits in stages_of(split)]
    half = split // 2
    for i, c in enumerate(orders[0]):
        block = (a0 if i < half else a1)[i % half].astype(F32)
        shrink_out[pl.ds(pl.multiple_of((mine ^ c) * 4 * part, 4 * part), 4 * part), :] = block
    for i, c in enumerate(orders[1]):
        block = (b0 if i < half else b1)[i % half].astype(F32)
        rows = pl.ds(pl.multiple_of((mine ^ c) * part, part), part)
        for k in range(4):
            columns = pl.ds(pl.multiple_of((me ^ k) * 512, 512), 512)
            expand_out[rows, columns] = block[k * part : (k + 1) * part]


def attention_place_kernel(
    place, a0, a1, b0, b1, joined_out, dense_out, bias_out, dense_bias_out, expand_bias_out, shrink_bias_out,
    gain1_out, shift1_out, gain2_out, shift2_out, vec_s, sum_s, bias_s, *, split,
):
    me, mine = place[0], place[1]
    part = 128 // split
    orders = [xor_order(bits) for bits in stages_of(split)]
    half = split // 2
    for number, pair in enumerate(((a0, a1), (b0, b1))):
        for i, c in enumerate(orders[number]):
            block = pair[i >= half][i % half].astype(F32)
            r = mine ^ c
            rows = pl.ds(pl.multiple_of(r * part, part), part)
            for local in range(2):
                k = 2 * number + local
                piece = block[local * part : (local + 1) * part]
                for third in range(3):
                    columns = pl.ds(pl.multiple_of(third * D + (me ^ k) * 128, 128), 128)
                    joined_out[rows, columns] = piece[:, third * 128 : (third + 1) * 128]
                dense_out[rows, k * 128 : (k + 1) * 128] = piece[:, 384:512]
            if number == 0:
                vec_s[r] = block[2 * part : 2 * part + 8]
    own = pl.ds(pl.multiple_of(me * 128, 128), 128)
    for line in range(4):
        sum_s[line : line + 1, :] = jnp.sum(vec_s[line][0:4], axis=0, keepdims=True)
    sum_s[6:7, :] = vec_s[6][0:1]
    for k in range(4):
        for third in range(3):
            columns = pl.ds(pl.multiple_of(third * D + (me ^ k) * 128, 128), 128)
            bias_s[0:1, columns] = vec_s[4][k : k + 1, third * 128 : (third + 1) * 128]
    for line, target in ((0, gain1_out), (1, shift1_out), (2, gain2_out), (3, shift2_out)):
        target[...] = sum_s[line : line + 1, own].reshape(128)
    bias_out[...] = bias_s[0:1, pl.ds(pl.multiple_of(me * 384, 128), 384)].reshape(384)
    expand_bias_out[...] = vec_s[5][0:1].reshape(512)
    dense_bias_out[...] = sum_s[6:7, own].reshape(128)
    shrink_bias_out[...] = sum_s[6:7, own].reshape(128)


def rope_table(length):
    half = ROT // 2
    freqs = (10000.0 ** (-2.0 * np.arange(half, dtype=np.float64) / ROT)).astype(np.float32)
    angles = np.arange(length, dtype=np.float32)[:, None] * freqs[None, :]
    cosine = np.ones((length, HEAD_DIM), np.float32)
    up = np.zeros((length, HEAD_DIM), np.float32)
    down = np.zeros((length, HEAD_DIM), np.float32)
    cosine[:, :half] = np.cos(angles)
    cosine[:, half:ROT] = np.cos(angles)
    up[:, :half] = -np.sin(angles)
    down[:, half:ROT] = np.sin(angles)
    return np.concatenate([np.tile(part, (1, 2)) for part in (cosine, up, down)], axis=1)


def per_device(
    tokens,
    cotangent,
    segments,
    pad_mask,
    slot_table,
    joined_weight,
    joined_bias,
    dense_weight,
    dense_bias,
    expand_weight,
    expand_bias,
    shrink_weight,
    shrink_bias,
    first_gain,
    first_shift,
    second_gain,
    second_shift,
):
    replicas = lax.axis_size("replica")
    me = lax.axis_index("shard")
    mine = lax.axis_index("replica")
    place = jnp.stack([me, mine]).astype(jnp.int32)
    part = 128 // replicas
    split = replicas if part % 16 == 0 and replicas >= 8 else 0
    params = pltpu.CompilerParams(vmem_limit_bytes=56 * 1024 * 1024)
    smem = pl.BlockSpec(memory_space=pltpu.SMEM)
    vmem = pl.BlockSpec(memory_space=pltpu.VMEM)
    shaped = jax.ShapeDtypeStruct

    def call(kernel, name, outs, scratch, *args):
        return pl.pallas_call(
            kernel,
            out_shape=tuple(outs),
            in_specs=[smem] + [vmem] * (len(args) - 1),
            out_specs=(vmem,) * len(outs),
            scratch_shapes=[pltpu.VMEM(*item) for item in scratch],
            compiler_params=params,
            name=name,
        )(*args)

    tok = tokens[0]
    tok_across = exchange(tok, "shard", 2)
    tok_near = exchange(tok, "shard", 1)

    live = slot_table[0][:, None] * pad_mask[0]
    seg = segments[0]
    code = jnp.where(live > 0, seg, -1)
    meta = jnp.concatenate(
        [
            jnp.concatenate([seg.reshape(256), code.reshape(256)]).astype(BF16)[None],
            jnp.concatenate([first_gain, first_shift, second_gain, second_shift])[None],
            jnp.pad(joined_bias, (0, 128))[None],
            jnp.zeros((META - 3, D), BF16),
        ],
        axis=0,
    )
    block = shaped((2, 128 + META, D), BF16)
    own, near_send, across_send = call(
        pack_kernel, "pack_weights", [block] * 3, [], place, joined_weight, expand_weight, meta
    )
    near = exchange(near_send, "shard", 1)
    across = exchange(across_send, "shard", 2)
    dy = jnp.where(live[:, :, None] > 0, cotangent[0], jnp.zeros((), BF16))
    dy_across = exchange(dy, "shard", 2)
    dy_near = exchange(dy, "shard", 1)
    beside = exchange(across, "replica", 1)
    far = exchange(jnp.stack([across[1], beside[1]]), "shard", 1)
    tok_far = exchange(tok_across, "shard", 1)
    dy_far = exchange(dy_across, "shard", 1)
    weights = (own, near, across, beside, far)
    toks = [item.reshape(256, D) for item in (tok, tok_near, tok_across, tok_far)]
    dys = [item.reshape(256, D) for item in (dy, dy_near, dy_across, dy_far)]

    def chunk_outs(rows_one, rows_other):
        one = shaped((replicas // 2, rows_one, D), BF16)
        other = shaped((replicas // 2, rows_other, D), BF16)
        return [one, one, other, other]

    orders = [jnp.asarray(xor_order(bits), jnp.int32) for bits in stages_of(replicas)]

    def halves(chunks, order):
        ordered = chunks[mine ^ order]
        return ordered[: replicas // 2], ordered[replicas // 2 :]

    def by_owner(pair, order):
        place_of = jnp.zeros((replicas,), jnp.int32).at[mine ^ order].set(jnp.arange(replicas, dtype=jnp.int32))
        return jnp.concatenate(pair, axis=0)[place_of]

    rows1024 = shaped((4, 2, 128, D), F32)
    vec_shape = shaped((8, D), F32)
    mlp, e_second, vec_mlp, *mlp_grads = call(
        functools.partial(mlp_kernel, split=split),
        "mlp_branch",
        [rows1024, rows1024, vec_shape]
        + (chunk_outs(4 * part, 4 * part) if split else [shaped((2, 512, D), BF16)]),
        [
            ((512, 512), BF16),
            ((4, META, D), F32),
            ((1024, D), BF16),
            ((1024, 512), BF16),
            ((1024, 512), BF16),
            ((1024, D), BF16),
            ((8, 64, D), BF16),
            ((8, 4, 16, D), BF16),
        ],
        place, *toks, *dys, *weights, shrink_weight, expand_bias.astype(F32).reshape(1, 512),
    )
    if not split:
        blocks = mlp_grads[0][1].reshape(4, replicas, part, D).transpose(1, 0, 2, 3)
        blocks = blocks[:, me ^ jnp.arange(4, dtype=jnp.int32)]
        mlp_grads = [
            *halves(mlp_grads[0][0].reshape(replicas, 4 * part, D), orders[0]),
            *halves(blocks.reshape(replicas, 4 * part, D), orders[1]),
        ]
    shrink_own, expand_own = scatter_sum(mlp_grads[0::2], mlp_grads[1::2], "replica")
    expand_own = expand_own.reshape(4, part, D)
    expand_own = jnp.concatenate(
        [expand_own[0:1]] + [exchange(expand_own[k : k + 1], "shard", k) for k in (1, 2, 3)], axis=0
    )
    mlp_done = gather_back(shrink_own, expand_own.reshape(4 * part, D), "replica")

    out_bias = (dense_bias.astype(F32) + shrink_bias.astype(F32)).reshape(1, 128)
    table = rope_table(4 * 128)
    half_rows = shaped((2, 2, 128, D), BF16)
    scratch = [
        ((512, 384), BF16),
        ((4, META, D), F32),
        ((8, 3 * D), F32),
        ((512, D), BF16),
        ((512, D), BF16),
        ((4, 2, 128, D), BF16),
        ((8, 5, 16, D), BF16),
    ]
    common = (place, *toks, *dys, *weights, dense_weight, out_bias, table, mlp, e_second)
    keep0, send0, joined_part, dense_part, vec_part = call(
        functools.partial(attention_kernel, slot=0, split=split),
        "attention_first_slot",
        [half_rows, half_rows, shaped((512, 384), F32), shaped((128, D), F32), vec_shape],
        scratch,
        *common, vec_mlp,
    )
    keep1, send1, *att_grads = call(
        functools.partial(attention_kernel, slot=1, split=split),
        "attention_second_slot",
        [half_rows, half_rows]
        + (chunk_outs(3 * part, 2 * part) if split else [shaped((4, 128, D), BF16), vec_shape]),
        scratch,
        *common, vec_part, joined_part, dense_part,
    )
    if not split:
        blocks = att_grads[0].reshape(4, replicas, part, D).transpose(1, 0, 2, 3)
        joined_blocks = blocks[:, me ^ jnp.arange(4, dtype=jnp.int32)][..., :384]
        blocks = jnp.concatenate([joined_blocks, blocks[..., 384:]], axis=3)
        line = jnp.pad(att_grads[1], ((0, replicas - 8), (0, 0))).astype(BF16)[:, None]
        att_grads = [
            *halves(jnp.concatenate([blocks[:, :2].reshape(replicas, 2 * part, D), line], axis=1), orders[0]),
            *halves(blocks[:, 2:].reshape(replicas, 2 * part, D), orders[1]),
        ]

    finished = []
    for slot, (keep, send) in enumerate(((keep0, send0), (keep1, send1))):
        total = keep.astype(F32) + exchange(send, "shard", 1).astype(F32)
        arrived = exchange(total[1].astype(BF16), "shard", 2)
        finished.append(
            pl.pallas_call(
                finish_kernel,
                out_shape=(shaped((128, D), BF16), shaped((128, D), F32)),
                in_specs=[vmem] * 4,
                out_specs=(vmem,) * 2,
                compiler_params=params,
                name="finish_rows",
            )(total[0], arrived, tok[slot], dy[slot])
        )
    output = jnp.stack([item[0] for item in finished])[None]
    input_grad = jnp.stack([item[1] for item in finished])[None]

    one, other = scatter_sum(att_grads[0::2], att_grads[1::2], "replica")
    blocks = jnp.concatenate([one[: 2 * part], other], axis=0).reshape(4, part, D)
    line = one[2 * part : 2 * part + 1]
    lines = jnp.broadcast_to(line, (16, D))
    moved = [
        exchange(jnp.concatenate([blocks[k], lines], axis=0), "shard", k) for k in (1, 2, 3)
    ]
    blocks = [blocks[0]] + [
        jnp.concatenate([item[:part, :384], blocks[k + 1][:, 384:]], axis=1) for k, item in enumerate(moved)
    ]
    lines = jnp.concatenate([line] + [item[part : part + 1] for item in moved] + [jnp.zeros((12, D), BF16)], axis=0)
    att_done = gather_back(
        jnp.concatenate([blocks[0], blocks[1], lines], axis=0),
        jnp.concatenate([blocks[2], blocks[3]], axis=0),
        "replica",
    )

    if split:
        grad_shrink, grad_expand = call(
            functools.partial(mlp_place_kernel, split=split),
            "place_mlp_grads",
            [shaped((512, D), F32), shaped((128, FF), F32)],
            [],
            place, *mlp_done[0], *mlp_done[1],
        )
        vectors = [384, 128, 512, 128, 128, 128, 128, 128]
        grad_joined, grad_dense, *vectors = call(
            functools.partial(attention_place_kernel, split=split),
            "place_attention_grads",
            [shaped((128, 3 * D), F32), shaped((128, D), F32)] + [shaped((width,), F32) for width in vectors],
            [((8, 8, D), F32), ((8, D), F32), ((8, 3 * D), F32)],
            place, *att_done[0], *att_done[1],
        )
    else:
        xor4 = me ^ jnp.arange(4, dtype=jnp.int32)
        shrink_all = by_owner(mlp_done[0], orders[0]).astype(F32)
        expand_all = by_owner(mlp_done[1], orders[1]).astype(F32).reshape(replicas, 4, part, D)[:, xor4]
        grad_shrink = shrink_all.reshape(512, D)
        grad_expand = expand_all.transpose(0, 2, 1, 3).reshape(128, FF)
        one = by_owner(att_done[0], orders[0]).astype(F32)
        other = by_owner(att_done[1], orders[1]).astype(F32)
        mats = jnp.concatenate([one[:, : 2 * part], other], axis=1).reshape(replicas, 4, part, D)
        grad_dense = mats[..., 384:].transpose(0, 2, 1, 3).reshape(128, D)
        grad_joined = (
            mats[:, xor4, :, :384].reshape(replicas, 4, part, 3, 128).transpose(0, 2, 3, 1, 4).reshape(128, 3 * D)
        )
        lines = one[:8, 2 * part : 2 * part + 4][:, xor4]
        summed = lax.dynamic_slice_in_dim(lines[:4].sum(axis=1), me * 128, 128, axis=1)
        bias_line = lines[4, :, :384].reshape(4, 3, 128).transpose(1, 0, 2).reshape(3 * D)
        dense_line = lax.dynamic_slice_in_dim(lines[6, me], me * 128, 128, axis=0)
        vectors = [
            lax.dynamic_slice_in_dim(bias_line, me * 384, 384, axis=0),
            dense_line,
            lines[5, me],
            dense_line,
            summed[0],
            summed[1],
            summed[2],
            summed[3],
        ]
    return (
        output,
        input_grad,
        grad_joined,
        vectors[0],
        grad_dense,
        vectors[1],
        grad_expand,
        vectors[2],
        grad_shrink,
        *vectors[3:],
    )


def solution(mesh):
    rows = P("replica", None, "shard", None)
    codes = P("replica", None, "shard")
    matrix = P("shard", None)
    vector = P("shard")
    return jax.shard_map(
        per_device,
        mesh=mesh,
        in_specs=(rows, rows, codes, codes, P("replica", None))
        + (matrix, vector) * 4
        + (vector,) * 4,
        out_specs=(rows, rows) + (matrix, vector) * 4 + (vector,) * 4,
        check_vma=False,
    )
```

```python
import functools

import jax
import jax.numpy as jnp
import numpy as np
from jax import lax
from jax.experimental import pallas as pl
from jax.experimental.pallas import tpu as pltpu
from jax.sharding import PartitionSpec as P

D = 512
HEADS = 8
HEAD_DIM = 64
FF = 2048
ROT = 16
META = 16
LINES = 16
PACKED = (
    ((128, 3 * D), jnp.bfloat16),
    ((128, FF), jnp.bfloat16),
    ((2, 128, D), jnp.bfloat16),
    ((2, 128), jnp.int32),
    ((2, 128), jnp.int32),
    ((384,), jnp.bfloat16),
) + (((128,), jnp.bfloat16),) * 4

F32 = jnp.float32
BF16 = jnp.bfloat16


def exchange(value, axis, bit):
    size = lax.axis_size(axis)
    return lax.ppermute(value, axis, [(i, i ^ bit) for i in range(size)])


def xor_order(bits):
    found = [0]
    for bit in reversed(bits):
        found = found + [number | bit for number in found]
    return found


def stages_of(size, core):
    bits = [1 << place for place in range(size.bit_length() - 1)]
    return bits if core == 0 else bits[1::-1] + bits[2:]


def replica_exchange(value, stage):
    replicas, shards = lax.axis_size("replica"), lax.axis_size("shard")
    pairs = []
    for replica in range(replicas):
        for shard in range(shards):
            other = replica ^ stages_of(replicas, shard % 2)[stage]
            pairs.append((replica * shards + shard, other * shards + shard))
    return lax.ppermute(value, ("replica", "shard"), pairs)


def tied(values, *others):
    leaves, tree = jax.tree.flatten(values)
    held = lax.optimization_barrier((*leaves, *jax.tree.leaves(others)))
    return jax.tree.unflatten(tree, held[: len(leaves)])


def dot(left, right):
    return jnp.dot(left, right, preferred_element_type=F32)


def dot_tb(left, right):
    return lax.dot_general(left, right, (((1,), (1,)), ((), ())), preferred_element_type=F32)


def dot_ta(left, right):
    return lax.dot_general(left, right, (((0,), (0,)), ((), ())), preferred_element_type=F32)


def chunk_index(me, size, skip):
    orders = [xor_order(stages_of(size, core)[skip:]) for core in (0, 1)]
    return [jnp.where(me % 2 == 0, one, other) for one, other in zip(*orders, strict=True)]


def first_bit(me, size):
    return jnp.where(me % 2 == 0, stages_of(size, 0)[0], stages_of(size, 1)[0])


def normalized(values):
    center = values - jnp.mean(values, axis=-1, keepdims=True)
    spread = jnp.mean(center * center, axis=-1, keepdims=True)
    root = lax.rsqrt(spread + 1e-05)
    return center * root, root


def pack_kernel(slots, *refs):
    count = len(PACKED)
    sources, (dy, near, expand_y, expand_d, joined_y, joined_d), targets = (
        refs[:count], refs[count : count + 6], refs[count + 6 : 2 * count + 6]
    )
    sems = refs[-1]
    copies = [pltpu.make_async_copy(*pair, sems.at[i]) for i, pair in enumerate(zip(sources, targets, strict=True))]
    for copy in copies:
        copy.start()
    for copy in copies:
        copy.wait()
    joined, expand, cot, seg, pad, joined_bias, *gain_refs = targets
    me, column = lax.axis_index("shard"), lax.axis_index("replica") % 2
    rows = []
    for s in range(2):
        live = pad[s : s + 1, :] * slots[0, s]
        code = jnp.where(live > 0, seg[s : s + 1, :], -1).astype(F32)
        rows.append((seg[s : s + 1, :].astype(F32), code))
        alive = jnp.transpose(jnp.broadcast_to(live.astype(F32), (8, 128)))[:, 0:1]
        dy[s * 128 : (s + 1) * 128, :] = jnp.where(alive > 0.0, cot[s].astype(F32), 0.0).astype(BF16)
    docs = jnp.concatenate([rows[0][0], rows[1][0], rows[0][1], rows[1][1]], axis=1)
    gains = jnp.concatenate([ref[...].astype(F32).reshape(1, 128) for ref in gain_refs], axis=1)
    bias = jnp.concatenate([joined_bias[...].astype(F32).reshape(1, 384), jnp.zeros((1, 128), F32)], axis=1)
    dy[256:, :] = jnp.concatenate([docs, gains, bias, jnp.zeros((META - 3, D), F32)], axis=0).astype(BF16)
    half = pl.ds(pl.multiple_of(column * 64, 64), 64)
    expand_y[...] = expand[half, pl.ds(pl.multiple_of((me ^ 2) * 512, 512), 512)]
    expand_d[...] = expand[half, pl.ds(pl.multiple_of((me ^ 3) * 512, 512), 512)]
    near[0] = expand[:, pl.ds(pl.multiple_of((me ^ 1) * 512, 512), 512)]
    copy_joined(joined, me ^ 1, near.at[1])
    near[1, :, 384:512] = jnp.zeros((128, 128), BF16)
    copy_joined(joined, me ^ 2, joined_y)
    copy_joined(joined, me ^ 3, joined_d)


def copy_kernel(source, target):
    target[...] = source[...]


def copy_joined(joined, j, target):
    for third in range(3):
        start = pl.multiple_of(third * D + j * 128, 128)
        target[0:128, third * 128 : (third + 1) * 128] = joined[:, pl.ds(start, 128)]


def meta_row(meta_s, line, start, stop):
    return jnp.concatenate([meta_s[j, line : line + 1, start:stop] for j in range(4)], axis=1)


def mlp_kernel(
    t0, t1, t2, t3, d0, d1, d2, d3, expand, near, expand_y, expand_d, expand_x, shrink, bias,
    mlp_out, e_out, vec_out, meta_s, *rest, split,
):
    outs, (expand_s, second_s, act_s, inner_s, dy_s, grad_s) = rest[:-6], rest[-6:]
    me, mine = lax.axis_index("shard"), lax.axis_index("replica")
    column = mine % 2
    for k, cot in enumerate((d0, d1, d2, d3)):
        meta_s[me ^ k] = cot[256:, :].astype(F32)

    def rows_of(k, start, size):
        return pl.ds(pl.multiple_of((me ^ k) * 128 + start, 64), size)

    expand_s[rows_of(0, 0, 128), :] = expand[:, pl.ds(pl.multiple_of(me * 512, 512), 512)]
    expand_s[rows_of(1, 0, 128), :] = near[0]
    for k, straight in ((2, expand_y), (3, expand_d)):
        expand_s[rows_of(k, column * 64, 64), :] = straight[...]
        expand_s[rows_of(k, (1 - column) * 64, 64), :] = expand_x[k - 2]
    gain = meta_row(meta_s, 1, 256, 384)
    shift = meta_row(meta_s, 1, 384, 512)
    vec_gain = jnp.zeros((1, D), F32)
    vec_shift = jnp.zeros((1, D), F32)
    vec_bias = jnp.zeros((1, 512), F32)
    vec_dy = jnp.zeros((1, D), F32)
    for k, (tok, cot) in enumerate(((t0, d0), (t1, d1), (t2, d2), (t3, d3))):
        rows = slice(k * 256, (k + 1) * 256)
        hat, _ = normalized(tok[...].astype(F32))
        second = (hat * gain + shift).astype(BF16)
        second_s[rows, :] = second
        inner = dot(second, expand_s[...]) + bias[...]
        half = 0.5 + 0.5 * lax.erf(inner * (0.5**0.5))
        act = (inner * half).astype(BF16)
        act_s[rows, :] = act
        slope = half + inner * jnp.exp(inner * inner * -0.5) * ((0.5 / np.pi) ** 0.5)
        dy = cot[0:256, :]
        dy_s[rows, :] = dy
        mlp_out[me ^ k] = dot(act, shrink[...]).reshape(2, 128, D)
        d_inner = (dot_tb(dy, shrink[...]) * slope).astype(BF16)
        inner_s[rows, :] = d_inner
        d_second = dot_tb(d_inner, expand_s[...])
        e_out[me ^ k] = (d_second * gain).reshape(2, 128, D)
        vec_gain += jnp.sum(d_second * hat, axis=0, keepdims=True)
        vec_shift += jnp.sum(d_second, axis=0, keepdims=True)
        vec_bias += jnp.sum(d_inner.astype(F32), axis=0, keepdims=True)
        vec_dy += jnp.sum(dy.astype(F32), axis=0, keepdims=True)
    vec_out[...] = jnp.zeros_like(vec_out)
    vec_out[2:3, :] = vec_gain
    vec_out[3:4, :] = vec_shift
    vec_out[5:6, :] = vec_bias
    vec_out[6:7, :] = vec_dy
    grad_shrink = dot_ta(act_s[...], dy_s[...]).astype(BF16)
    grad_expand = dot_ta(second_s[...], inner_s[...]).astype(BF16)
    if not split:
        outs[0][0] = grad_shrink
        outs[0][1] = grad_expand
        return
    part = 128 // split
    grad_s[:, 0:4] = grad_shrink.reshape(split, 4, part, D)
    for j in range(4):
        grad_s[:, 4 + (me ^ j)] = grad_expand[j * 128 : (j + 1) * 128].reshape(split, part, D)
    for i, c in enumerate(chunk_index(me, split, 1)):
        outs[0][i] = grad_s[mine ^ c].reshape(8 * part, D)
        outs[1][i] = grad_s[mine ^ c ^ first_bit(me, split)].reshape(8 * part, D)


def turned(values, cosine, sine_up, sine_down, sign):
    up = pltpu.roll(values, 120, 1)
    down = pltpu.roll(values, 8, 1)
    return values * cosine + (up * sine_up + down * sine_down) * sign


def attention_kernel(
    t0, t1, t2, t3, d0, d1, d2, d3, meta_s, dense, dense_bias, shrink_bias, table, mlp, e_in, vec_in, *rest,
    slot, split,
):
    s = slot
    if s == 0:
        (joined, near, joined_y, joined_d), rest = rest[:4], rest[4:]
        (keep_out, send_out, joined_out, dense_out, vec_out, joined_w), rest = rest[:6], rest[6:]
    else:
        (joined_in, dense_in, joined_w), rest = rest[:3], rest[3:]
        (keep_out, send_out), rest = rest[:2], rest[2:]
    outs, (bias_s, tok_s, dy_s, both_s, grad_s) = rest[:-5], rest[-5:]
    if s == 0:
        me = lax.axis_index("shard")
        copy_joined(joined, me, joined_w.at[pl.ds(pl.multiple_of(me * 128, 128), 128)])
        for k, block in ((1, near.at[1]), (2, joined_y), (3, joined_d)):
            joined_w[pl.ds(pl.multiple_of((me ^ k) * 128, 128), 128), :] = block[:, 0:384]
    me, mine = lax.axis_index("shard"), lax.axis_index("replica")
    for k, (tok, cot) in enumerate(((t0, d0), (t1, d1), (t2, d2), (t3, d3))):
        start = pl.multiple_of((me ^ k) * 128, 128)
        tok_s[pl.ds(start, 128), :] = tok[s * 128 : (s + 1) * 128, :]
        dy_s[pl.ds(start, 128), :] = cot[s * 128 : (s + 1) * 128, :]
    gain = meta_row(meta_s, 1, 0, 128)
    shift = meta_row(meta_s, 1, 128, 256)
    bias_s[0:1, :] = meta_row(meta_s, 2, 0, 384)
    joined_bias = jnp.concatenate(
        [bias_s[0:1, pl.ds(pl.multiple_of(part * D + me * 128, 128), 128)] for part in range(3)], axis=1
    )
    low_half = lax.broadcasted_iota(jnp.int32, (1, 128), 1) < HEAD_DIM
    cosine = table[:, 0:128]
    sine_up = table[:, 128:256]
    sine_down = table[:, 256:384]
    zero = jnp.zeros((), BF16)
    hat, _ = normalized(tok_s[...].astype(F32))
    first = (hat * gain + shift).astype(BF16)
    joined = dot(first, joined_w[...]) + joined_bias
    query = (turned(joined[:, 0:128], cosine, sine_up, sine_down, 1.0) * (HEAD_DIM**-0.5)).astype(BF16)
    key = turned(joined[:, 128:256], cosine, sine_up, sine_down, 1.0).astype(BF16)
    value = joined[:, 256:384].astype(BF16)
    dy = dy_s[...]
    d_heads = dot_tb(dy, dense[...]).astype(BF16)
    query_doc = jnp.transpose(
        jnp.broadcast_to(meta_row(meta_s, 0, s * 128, (s + 1) * 128), (8, 512))
    )[:, 0:1]
    key_doc = meta_row(meta_s, 0, 256 + s * 128, 256 + (s + 1) * 128)
    query_grads = []
    heads_parts = []
    key_grad = jnp.zeros((128, 512), F32)
    value_grad = jnp.zeros((128, 512), F32)
    for block in range(2):
        lo, hi = block * 256, (block + 1) * 256
        at = lax.broadcasted_iota(jnp.int32, (256, hi), 0) + lo
        to = lax.broadcasted_iota(jnp.int32, (256, hi), 1)
        allowed = ((query_doc[lo:hi] == key_doc[:, :hi]) & (to <= at)) | (to == at)
        out = jnp.zeros((256, 128), F32)
        query_grad = jnp.zeros((256, 128), F32)
        key_part = jnp.zeros((128, hi), F32)
        value_part = jnp.zeros((128, hi), F32)
        for h in range(2):
            ours = low_half if h == 0 else jnp.logical_not(low_half)
            q_h = jnp.where(ours, query[lo:hi], zero)
            k_h = jnp.where(ours, key[:hi], zero)
            v_h = jnp.where(ours, value[:hi], zero)
            g_h = jnp.where(ours, d_heads[lo:hi], zero)
            scores = jnp.where(allowed, dot_tb(q_h, k_h), -1e30)
            top = jnp.max(scores, axis=-1, keepdims=True)
            expd = jnp.exp(scores - top)
            probs = expd * (1.0 / jnp.sum(expd, axis=-1, keepdims=True))
            probs_low = probs.astype(BF16)
            out += dot(probs_low, v_h)
            d_probs = dot_tb(g_h, v_h)
            weighted = d_probs * probs
            d_scores = (weighted - probs * jnp.sum(weighted, axis=-1, keepdims=True)).astype(BF16)
            query_grad += dot(d_scores, k_h)
            key_part += dot_ta(q_h, d_scores)
            value_part += dot_ta(g_h, probs_low)
        query_grads.append(query_grad)
        heads_parts.append(out)
        if hi < 512:
            pad = jnp.zeros((128, 512 - hi), F32)
            key_part = jnp.concatenate([key_part, pad], axis=1)
            value_part = jnp.concatenate([value_part, pad], axis=1)
        key_grad += key_part
        value_grad += value_part
    heads = jnp.concatenate(heads_parts, axis=0).astype(BF16)
    query_grad = jnp.concatenate(query_grads, axis=0) * (HEAD_DIM**-0.5)
    d_joined = jnp.concatenate(
        [
            turned(query_grad, cosine, sine_up, sine_down, -1.0),
            turned(jnp.transpose(key_grad), cosine, sine_up, sine_down, -1.0),
            jnp.transpose(value_grad),
        ],
        axis=1,
    ).astype(BF16)
    d_first = dot_tb(d_joined, joined_w[...])
    grad_in = d_first * gain
    own_columns = lax.broadcasted_iota(jnp.int32, (1, D), 1) // 128 == me
    out_bias = dense_bias[...] + shrink_bias[...]
    attention = dot(heads, dense[...]) + jnp.where(own_columns, jnp.concatenate([out_bias] * 4, axis=1), 0.0)
    for j in range(4):
        piece = slice(j * 128, (j + 1) * 128)
        both_s[j, 0] = (attention[piece] + mlp[j, s]).astype(BF16)
        both_s[j, 1] = (grad_in[piece] + e_in[j, s]).astype(BF16)
    for i in range(2):
        keep_out[i] = both_s[me ^ (2 * i)]
        send_out[i] = both_s[me ^ (2 * i + 1)]
    grad_joined = dot_ta(first, d_joined)
    grad_dense = dot_ta(heads, dy)
    vec = vec_in[...]
    line = lax.broadcasted_iota(jnp.int32, (8, D), 0)
    vec = vec + jnp.where(line == 0, jnp.sum(d_first * hat, axis=0, keepdims=True), 0.0)
    vec = vec + jnp.where(line == 1, jnp.sum(d_first, axis=0, keepdims=True), 0.0)
    bias_line = jnp.concatenate(
        [jnp.sum(d_joined.astype(F32), axis=0, keepdims=True), jnp.zeros((1, 128), F32)], axis=1
    )
    vec = vec + jnp.where(line == 4, bias_line, 0.0)
    if s == 0:
        joined_out[...] = grad_joined
        dense_out[...] = grad_dense
        vec_out[...] = vec
        return
    grad_joined = (grad_joined + joined_in[...]).astype(BF16)
    grad_dense = (grad_dense + dense_in[...]).astype(BF16)
    if not split:
        for j in range(4):
            outs[0][j, :, 0:384] = grad_joined[j * 128 : (j + 1) * 128]
            outs[0][j, :, 384:512] = grad_dense[:, j * 128 : (j + 1) * 128]
        outs[1][...] = vec
        return
    part = 128 // split
    for j in range(4):
        grad_s[:, me ^ j, :, 0:384] = grad_joined[j * 128 : (j + 1) * 128].reshape(split, part, 384)
        grad_s[:, j, :, 384:512] = grad_dense[:, j * 128 : (j + 1) * 128].reshape(split, part, 128)
    for r in range(split):
        grad_s[r, 4] = jnp.broadcast_to(vec[r % 8 : r % 8 + 1], (part, D)).astype(BF16)
    for i, c in enumerate(chunk_index(me, split, 1)):
        outs[0][i] = grad_s[mine ^ c].reshape(4 * part + LINES, D)
        outs[1][i] = grad_s[mine ^ c ^ first_bit(me, split)].reshape(4 * part + LINES, D)


def rows_kernel(keep0, keep1, near0, near1, own, send):
    for slot, (keep, near) in enumerate(((keep0, near0), (keep1, near1))):
        own[slot] = keep[0].astype(F32) + near[0].astype(F32)
        send[slot] = (keep[1].astype(F32) + near[1].astype(F32)).astype(BF16)


def fold_kernel(keep, arrived, kept, send):
    half = kept.shape[0]
    for i in range(half):
        kept[i] = keep[i].astype(F32) + arrived[i].astype(F32)
        send[i] = (keep[half + i].astype(F32) + arrived[half + i].astype(F32)).astype(BF16)


def fold_last_kernel(keep, arrived, total):
    total[...] = (keep[...].astype(F32) + arrived[...].astype(F32)).astype(BF16)


def join_kernel(one, other, out):
    out[0] = one[1]
    out[1] = other[1]


def concat_kernel(held, arrived, out):
    size = held.shape[0]
    out[0:size] = held[...]
    out[size:] = arrived[...]


def mlp_cut_kernel(keep, arrived, shrink, stay, send, *, part):
    total = (keep[0].astype(F32) + arrived[0].astype(F32)).astype(BF16)
    shrink[...] = total[: 4 * part]
    for k in range(4):
        (stay, send)[k % 2][k // 2] = total[(4 + k) * part : (5 + k) * part]


def mlp_arrange_kernel(shrink, stay, near, across, held, *, part):
    held[0, : 4 * part] = shrink[...]
    for k, item in enumerate((stay.at[0], near.at[0], across.at[0], across.at[1])):
        held[0, (4 + k) * part : (5 + k) * part] = item[...]


def middle_kernel(pair, arrived, stay, send, *, part):
    total = [(pair[c].astype(F32) + arrived[1 - c].astype(F32)).astype(BF16) for c in range(2)]
    line = jnp.concatenate(
        [total[c][4 * part :].astype(F32)[0:1] for c in range(2)] + [jnp.zeros((LINES - 2, D), F32)], axis=0
    ).astype(BF16)
    for k in range(4):
        target = (stay, send)[k % 2]
        for c in range(2):
            target[k // 2, c * part : (c + 1) * part, :] = total[c][k * part : (k + 1) * part]
        target[k // 2, 2 * part :, :] = line


def arrange_kernel(stay, send, near, across, held, *, part):
    moved = (stay.at[0], near.at[0], across.at[0], across.at[1])
    for c in range(2):
        rows = slice(c * part, (c + 1) * part)
        for k in range(4):
            held[c, k * part : (k + 1) * part, 0:384] = moved[k][rows, 0:384]
            held[c, k * part : (k + 1) * part, 384:512] = (stay, send)[k % 2][k // 2, rows, 384:512]
        lines = [item[2 * part :, :].astype(F32)[c : c + 1] for item in moved]
        held[c, 4 * part :, :] = jnp.concatenate(lines + [jnp.zeros((LINES - 4, D), F32)], axis=0).astype(BF16)


def finish_kernel(keep, arrived, tok, cot, out, grad):
    for slot in range(2):
        tokens = tok[slot].astype(F32)
        out[slot] = (tokens + keep[slot, 0] + arrived[slot, 0].astype(F32)).astype(BF16)
        e = keep[slot, 1] + arrived[slot, 1].astype(F32)
        hat, root = normalized(tokens)
        mean_e = jnp.mean(e, axis=-1, keepdims=True)
        mean_eh = jnp.mean(e * hat, axis=-1, keepdims=True)
        grad[slot] = cot[slot * 128 : (slot + 1) * 128, :].astype(F32) + root * (e - mean_e - hat * mean_eh)


def mlp_place_kernel(held, arrived, shrink_out, expand_out, *, split):
    me, mine = lax.axis_index("shard"), lax.axis_index("replica")
    part = 128 // split
    half = split // 2
    for i, c in enumerate(chunk_index(me, split, 0)):
        block = (held if i < half else arrived)[i % half].astype(F32)
        shrink_out[pl.ds(pl.multiple_of((mine ^ c) * 4 * part, 4 * part), 4 * part), :] = block[: 4 * part]
        rows = pl.ds(pl.multiple_of((mine ^ c) * part, part), part)
        for k in range(4):
            columns = pl.ds(pl.multiple_of((me ^ k) * 512, 512), 512)
            expand_out[rows, columns] = block[(4 + k) * part : (5 + k) * part]


def attention_place_kernel(
    held, arrived, joined_out, dense_out, bias_out, dense_bias_out, expand_bias_out, shrink_bias_out,
    gain1_out, shift1_out, gain2_out, shift2_out, vec_s, sum_s, bias_s, *, split,
):
    me, mine = lax.axis_index("shard"), lax.axis_index("replica")
    part = 128 // split
    half = split // 2
    for i, c in enumerate(chunk_index(me, split, 0)):
        block = (held if i < half else arrived)[i % half].astype(F32)
        r = mine ^ c
        rows = pl.ds(pl.multiple_of(r * part, part), part)
        for k in range(4):
            piece = block[k * part : (k + 1) * part]
            for third in range(3):
                columns = pl.ds(pl.multiple_of(third * D + (me ^ k) * 128, 128), 128)
                joined_out[rows, columns] = piece[:, third * 128 : (third + 1) * 128]
            dense_out[rows, k * 128 : (k + 1) * 128] = piece[:, 384:512]
        vec_s[r] = block[4 * part : 4 * part + 8]
    own = pl.ds(pl.multiple_of(me * 128, 128), 128)
    for line in range(4):
        sum_s[line : line + 1, :] = jnp.sum(vec_s[line][0:4], axis=0, keepdims=True)
    sum_s[6:7, :] = vec_s[6][0:1]
    for k in range(4):
        for third in range(3):
            columns = pl.ds(pl.multiple_of(third * D + (me ^ k) * 128, 128), 128)
            bias_s[0:1, columns] = vec_s[4][k : k + 1, third * 128 : (third + 1) * 128]
    for line, target in ((0, gain1_out), (1, shift1_out), (2, gain2_out), (3, shift2_out)):
        target[...] = sum_s[line : line + 1, own].reshape(128)
    bias_out[...] = bias_s[0:1, pl.ds(pl.multiple_of(me * 384, 128), 384)].reshape(384)
    expand_bias_out[...] = vec_s[5][0:1].reshape(512)
    dense_bias_out[...] = sum_s[6:7, own].reshape(128)
    shrink_bias_out[...] = sum_s[6:7, own].reshape(128)


def rope_table(length):
    half = ROT // 2
    freqs = (10000.0 ** (-2.0 * np.arange(half, dtype=np.float64) / ROT)).astype(np.float32)
    angles = np.arange(length, dtype=np.float32)[:, None] * freqs[None, :]
    cosine = np.ones((length, HEAD_DIM), np.float32)
    up = np.zeros((length, HEAD_DIM), np.float32)
    down = np.zeros((length, HEAD_DIM), np.float32)
    cosine[:, :half] = np.cos(angles)
    cosine[:, half:ROT] = np.cos(angles)
    up[:, :half] = -np.sin(angles)
    down[:, half:ROT] = np.sin(angles)
    return np.concatenate([np.tile(part, (1, 2)) for part in (cosine, up, down)], axis=1)


def per_device(
    tokens,
    cotangent,
    segments,
    pad_mask,
    slot_table,
    joined_weight,
    joined_bias,
    dense_weight,
    dense_bias,
    expand_weight,
    expand_bias,
    shrink_weight,
    shrink_bias,
    first_gain,
    first_shift,
    second_gain,
    second_shift,
):
    replicas = lax.axis_size("replica")
    me = lax.axis_index("shard")
    mine = lax.axis_index("replica")
    part = 128 // replicas
    split = replicas if part % 16 == 0 and replicas >= 8 else 0
    steps = replicas.bit_length() - 1
    smem = pl.BlockSpec(memory_space=pltpu.SMEM)
    vmem = pl.BlockSpec(memory_space=pltpu.VMEM)
    shaped = jax.ShapeDtypeStruct

    def call(kernel, name, *, work, outs, scratch, args, limit=12):
        return pl.pallas_call(
            kernel,
            cost_estimate=pl.CostEstimate(flops=work, bytes_accessed=work // 300, transcendentals=0),
            out_shape=tuple(outs),
            in_specs=[vmem] * len(args),
            out_specs=(vmem,) * len(outs),
            scratch_shapes=[pltpu.VMEM(*item) for item in scratch],
            compiler_params=pltpu.CompilerParams(vmem_limit_bytes=limit * 1024 * 1024),
            name=name,
        )(*args)

    small = functools.partial(call, work=1000, scratch=[], limit=8)

    tok = tokens[0].reshape(256, D)
    tok_across = exchange(tok, "shard", 2)
    tok_near = exchange(tok, "shard", 1)
    half_block, joined_block = shaped((64, D), BF16), shaped((128, 384), BF16)
    dy, near_send, expand_y, expand_d, joined_y, joined_d = pl.pallas_call(
        pack_kernel,
        cost_estimate=pl.CostEstimate(flops=2 * 10**9, bytes_accessed=6 * 10**6, transcendentals=0),
        out_shape=(
            shaped((256 + META, D), BF16), shaped((2, 128, D), BF16), half_block, half_block, joined_block, joined_block
        ),
        in_specs=[smem] + [pl.BlockSpec(memory_space=pltpu.HBM)] * len(PACKED),
        out_specs=(vmem,) * 6,
        scratch_shapes=[pltpu.VMEM(*item) for item in PACKED] + [pltpu.SemaphoreType.DMA((len(PACKED),))],
        compiler_params=pltpu.CompilerParams(vmem_limit_bytes=60 * 1024 * 1024),
        name="pack_weights",
    )(
        slot_table, joined_weight, expand_weight, cotangent[0], segments[0], pad_mask[0], joined_bias,
        first_gain, first_shift, second_gain, second_shift,
    )
    near = exchange(near_send, "shard", 1)
    expand_y = exchange(expand_y, "shard", 2)
    expand_d = exchange(expand_d, "shard", 3)
    dy_near = exchange(dy, "shard", 1)
    dy_across = exchange(tied(dy, expand_y, expand_d, tok_across), "shard", 2)
    (dy_own,) = small(copy_kernel, "hold_rows", outs=[shaped(dy.shape, BF16)], args=(dy,))
    expand_x = exchange(tied(jnp.stack([expand_y, expand_d]), dy_own), "replica", 1)
    joined_y, joined_d = tied((joined_y, joined_d), dy_across)
    joined_y = exchange(joined_y, "shard", 2)
    joined_d = exchange(joined_d, "shard", 3)
    tok_far = exchange(tok_across, "shard", 1)
    dy_far = exchange(dy_across, "shard", 1)
    toks = (tok, tok_near, tok_across, tok_far)
    dys = (dy_own, dy_near, dy_across, dy_far)

    xor4 = me ^ jnp.arange(4, dtype=jnp.int32)
    order = jnp.where(me % 2 == 0, *[jnp.asarray(xor_order(stages_of(replicas, core)), jnp.int32) for core in (0, 1)])

    def halves(chunks):
        ordered = chunks[mine ^ order]
        return [ordered[: replicas // 2], ordered[replicas // 2 :]]

    def by_owner(pair):
        place_of = jnp.zeros((replicas,), jnp.int32).at[mine ^ order].set(jnp.arange(replicas, dtype=jnp.int32))
        return jnp.concatenate(pair, axis=0)[place_of].astype(F32)

    rows1024 = shaped((4, 2, 128, D), F32)
    vec_shape = shaped((8, D), F32)
    mlp, e_second, vec_mlp, meta_all, *mlp_state = call(
        functools.partial(mlp_kernel, split=split),
        "mlp_branch",
        work=6 * 10**9,
        outs=[rows1024, rows1024, vec_shape, shaped((4, META, D), F32)]
        + ([shaped((replicas // 2, 8 * part, D), BF16)] * 2 if split else [shaped((2, 512, D), BF16)]),
        scratch=[
            ((512, 512), BF16),
            ((1024, D), BF16),
            ((1024, 512), BF16),
            ((1024, 512), BF16),
            ((1024, D), BF16),
            ((8, 8, 16, D), BF16),
        ],
        args=(*toks, *dys, expand_weight, near, expand_y, expand_d, expand_x, shrink_weight, expand_bias.astype(F32).reshape(1, 512)),
    )
    if not split:
        blocks = mlp_state[0][1].reshape(4, replicas, part, D).transpose(1, 0, 2, 3)[:, xor4]
        mlp_state = halves(
            jnp.concatenate(
                [mlp_state[0][0].reshape(replicas, 4 * part, D), blocks.reshape(replicas, 4 * part, D)], axis=1
            )
        )
    def fold(state, stage, last=False, after=()):
        keep, send = state
        arrived = replica_exchange(tied(send, *after), stage)
        chunks = keep.shape
        half = shaped((chunks[0] // 2, *chunks[1:]), F32), shaped((chunks[0] // 2, *chunks[1:]), BF16)
        if split and last:
            return small(fold_last_kernel, "fold", outs=[shaped(chunks, BF16)], args=(keep, arrived))[0]
        if split:
            return small(fold_kernel, "fold", outs=half, args=(keep, arrived))
        total = keep.astype(F32) + arrived.astype(F32)
        if last:
            return total.astype(BF16)
        return total[: chunks[0] // 2], total[chunks[0] // 2 :].astype(BF16)

    def middle(pair):
        return replica_exchange(pair, steps - 1)

    def double(held, stage, *after):
        arrived = tied(replica_exchange(held, stage), *after)
        if split:
            whole = shaped((2 * held.shape[0], *held.shape[1:]), BF16)
            return small(concat_kernel, "double", outs=[whole], args=(held, arrived))[0]
        return jnp.concatenate([held, arrived], axis=0)

    def across_y(stay, near):
        if split:
            (both,) = small(join_kernel, "to_send_across", outs=[shaped(stay.shape, BF16)], args=(stay, near))
        else:
            both = jnp.stack([stay[1], near[1]])
        return exchange(both, "shard", 2)

    mlp_state = fold(mlp_state, 0)

    half_rows = shaped((2, 2, 128, D), BF16)
    scratch = [
        ((8, 3 * D), F32),
        ((512, D), BF16),
        ((512, D), BF16),
        ((4, 2, 128, D), BF16),
        ((8, 5, 16, D), BF16),
    ]
    common = (
        *toks, *dys, meta_all, dense_weight,
        dense_bias.astype(F32).reshape(1, 128), shrink_bias.astype(F32).reshape(1, 128),
        rope_table(4 * 128), mlp, e_second,
    )
    keep0, send0, joined_part, dense_part, vec_part, joined_all = call(
        functools.partial(attention_kernel, slot=0, split=split),
        "attention_first_slot",
        work=6 * 10**9,
        outs=[half_rows, half_rows, shaped((512, 384), F32), shaped((128, D), F32), vec_shape, shaped((512, 384), BF16)],
        scratch=scratch,
        args=(*common, vec_mlp, joined_weight, near, joined_y, joined_d),
    )
    keep1, send1, *att_state = call(
        functools.partial(attention_kernel, slot=1, split=split),
        "attention_second_slot",
        work=6 * 10**9,
        outs=[half_rows, half_rows]
        + ([shaped((replicas // 2, 4 * part + LINES, D), BF16)] * 2 if split else [shaped((4, 128, D), BF16), vec_shape]),
        scratch=scratch,
        args=(*common, tied(vec_part, mlp_state[1]), joined_part, dense_part, joined_all),
    )
    if not split:
        blocks = att_state[0].reshape(4, replicas, part, D).transpose(1, 0, 2, 3)
        blocks = jnp.concatenate([blocks[:, xor4][..., :384], blocks[..., 384:]], axis=3)
        line = jnp.pad(att_state[1], ((0, replicas - 8), (0, 0))).astype(BF16)[:, None]
        line = jnp.broadcast_to(line, (replicas, LINES, D))
        att_state = halves(jnp.concatenate([blocks.reshape(replicas, 4 * part, D), line], axis=1))

    for stage in range(1, steps - 1):
        mlp_state = fold(mlp_state, stage)

    mlp_new = replica_exchange(mlp_state[1], steps - 1)
    att_state = fold(att_state, 0, False, mlp_state)
    mlp_new = tied(mlp_new, att_state)
    if split:
        cut = shaped((2, part, D), BF16)
        shrink, mlp_stay, mlp_send = small(
            functools.partial(mlp_cut_kernel, part=part),
            "cut_mlp_grads",
            outs=[shaped((4 * part, D), BF16), cut, cut],
            args=(mlp_state[0], mlp_new),
        )
    else:
        mlp_sum = (mlp_state[0][0] + mlp_new[0].astype(F32)).astype(BF16)
        shrink = mlp_sum[: 4 * part]
        cuts = [mlp_sum[(4 + k) * part : (5 + k) * part] for k in range(4)]
        mlp_stay, mlp_send = jnp.stack([cuts[0], cuts[2]]), jnp.stack([cuts[1], cuts[3]])
    att_pair = att_state
    for stage in range(1, steps - 1):
        att_pair = fold(att_pair, stage, stage == steps - 2, (mlp_send,) if stage == 1 else ())
    mlp_near = exchange(mlp_send, "shard", 1)
    mlp_across = across_y(mlp_stay, mlp_near)
    if split:
        (mlp_held,) = small(
            functools.partial(mlp_arrange_kernel, part=part),
            "arrange_mlp_grads",
            outs=[shaped((1, 8 * part, D), BF16)],
            args=(shrink, mlp_stay, mlp_near, mlp_across),
        )
    else:
        mlp_held = jnp.concatenate([shrink, mlp_stay[0], mlp_near[0], mlp_across[0], mlp_across[1]], axis=0)[None]

    att_pair = tied(att_pair, mlp_held)
    att_new = middle(att_pair)

    from_near = [exchange(tied(send, att_pair), "shard", 1) for send in (send0, send1)]
    rows_own, rows_send = small(
        rows_kernel,
        "rows_between_cores",
        outs=[shaped((2, 2, 128, D), F32), shaped((2, 2, 128, D), BF16)],
        args=(keep0, keep1, *from_near),
    )

    if split:
        cut = shaped((2, 2 * part + LINES, D), BF16)
        stay, near_send = small(
            functools.partial(middle_kernel, part=part), "cut_attention_grads", outs=[cut, cut], args=(att_pair, att_new)
        )
    else:
        att_sum = (att_pair.astype(F32) + att_new[::-1].astype(F32)).astype(BF16)
        line = jnp.pad(att_sum[:, 4 * part], ((0, LINES - 2), (0, 0)))
        cuts = [
            jnp.concatenate([att_sum[:, k * part : (k + 1) * part].reshape(2 * part, D), line], axis=0) for k in range(4)
        ]
        stay, near_send = jnp.stack([cuts[0], cuts[2]]), jnp.stack([cuts[1], cuts[3]])
    near = exchange(near_send, "shard", 1)
    across = across_y(stay, near)
    if split:
        (att_held,) = small(
            functools.partial(arrange_kernel, part=part),
            "arrange_attention_grads",
            outs=[shaped((2, 4 * part + LINES, D), BF16)],
            args=(stay, near_send, near, across),
        )
    else:
        moved = [stay[0], near[0], across[0], across[1]]
        kept = [stay[0], near_send[0], stay[1], near_send[1]]
        mixed = [
            jnp.concatenate([item[: 2 * part, :384], same[: 2 * part, 384:]], axis=1).reshape(2, part, D)
            for item, same in zip(moved, kept, strict=True)
        ]
        lines = [item[2 * part : 2 * part + 2].reshape(2, 1, D) for item in moved]
        att_held = jnp.concatenate([*mixed, *lines, jnp.zeros((2, LINES - 4, D), BF16)], axis=1)

    arrived = exchange(tied(rows_send, att_held), "shard", 2)
    output, input_grad = small(
        finish_kernel,
        "finish_rows",
        outs=[shaped((2, 128, D), BF16), shaped((2, 128, D), F32)],
        args=(rows_own, arrived, tokens[0], dy_own),
    )

    mlp_held = double(tied(mlp_held, stay), steps - 1, att_held)
    for stage in reversed(range(1, steps - 1)):
        mlp_held = double(mlp_held, stage)
        att_held = double(att_held, stage)
    mlp_done = mlp_held, replica_exchange(mlp_held, 0)
    att_done = att_held, replica_exchange(att_held, 0)

    if split:
        grad_shrink, grad_expand = small(
            functools.partial(mlp_place_kernel, split=split),
            "place_mlp_grads",
            outs=[shaped((512, D), F32), shaped((128, FF), F32)],
            args=mlp_done,
        )
        widths = [384, 128, 512, 128, 128, 128, 128, 128]
        grad_joined, grad_dense, *vectors = call(
            functools.partial(attention_place_kernel, split=split),
            "place_attention_grads",
            work=1000,
            outs=[shaped((128, 3 * D), F32), shaped((128, D), F32)] + [shaped((width,), F32) for width in widths],
            scratch=[((8, 8, D), F32), ((8, D), F32), ((8, 3 * D), F32)],
            args=(att_done[0], tied(att_done[1], grad_shrink, output)),
            limit=8,
        )
    else:
        mlp_all, att_all = by_owner(mlp_done), by_owner(att_done)
        grad_shrink = mlp_all[:, : 4 * part].reshape(512, D)
        blocks = mlp_all[:, 4 * part :].reshape(replicas, 4, part, D)[:, xor4]
        grad_expand = blocks.transpose(0, 2, 1, 3).reshape(128, FF)
        blocks = att_all[:, : 4 * part].reshape(replicas, 4, part, D)
        grad_dense = blocks[..., 384:].transpose(0, 2, 1, 3).reshape(128, D)
        blocks = blocks[:, xor4, :, :384].reshape(replicas, 4, part, 3, 128)
        grad_joined = blocks.transpose(0, 2, 3, 1, 4).reshape(128, 3 * D)
        lines = att_all[:8, 4 * part : 4 * part + 4][:, xor4]
        summed = lax.dynamic_slice_in_dim(lines[:4].sum(axis=1), me * 128, 128, axis=1)
        bias_line = lines[4, :, :384].reshape(4, 3, 128).transpose(1, 0, 2).reshape(3 * D)
        dense_line = lax.dynamic_slice_in_dim(lines[6, me], me * 128, 128, axis=0)
        vectors = [
            lax.dynamic_slice_in_dim(bias_line, me * 384, 384, axis=0),
            dense_line,
            lines[5, me],
            dense_line,
            summed[0],
            summed[1],
            summed[2],
            summed[3],
        ]
    return (
        output[None],
        input_grad[None],
        grad_joined,
        vectors[0],
        grad_dense,
        vectors[1],
        grad_expand,
        vectors[2],
        grad_shrink,
        *vectors[3:],
    )


def solution(mesh):
    rows = P("replica", None, "shard", None)
    codes = P("replica", None, "shard")
    matrix = P("shard", None)
    vector = P("shard")
    return jax.shard_map(
        per_device,
        mesh=mesh,
        in_specs=(rows, rows, codes, codes, P("replica", None))
        + (matrix, vector) * 4
        + (vector,) * 4,
        out_specs=(rows, rows) + (matrix, vector) * 4 + (vector,) * 4,
        check_vma=False,
    )
```

```python
import functools

import jax
import jax.numpy as jnp
import numpy as np
from jax import lax
from jax.experimental import pallas as pl
from jax.experimental.pallas import tpu as pltpu
from jax.sharding import PartitionSpec as P

D = 512
HEADS = 8
HEAD_DIM = 64
FF = 2048
ROT = 16
META = 16
LINES = 16
PACKED = (
    ((128, 3 * D), jnp.bfloat16),
    ((128, FF), jnp.bfloat16),
    ((2, 128, D), jnp.bfloat16),
    ((2, 128), jnp.int32),
    ((2, 128), jnp.int32),
    ((384,), jnp.bfloat16),
) + (((128,), jnp.bfloat16),) * 4

F32 = jnp.float32
BF16 = jnp.bfloat16


def exchange(value, axis, bit):
    size = lax.axis_size(axis)
    return lax.ppermute(value, axis, [(i, i ^ bit) for i in range(size)])


def xor_order(bits):
    found = [0]
    for bit in reversed(bits):
        found = found + [number | bit for number in found]
    return found


def stages_of(size, core):
    bits = [1 << place for place in range(size.bit_length() - 1)]
    return bits if core == 0 else bits[1::-1] + bits[2:]


def replica_exchange(value, stage):
    replicas, shards = lax.axis_size("replica"), lax.axis_size("shard")
    pairs = []
    for replica in range(replicas):
        for shard in range(shards):
            other = replica ^ stages_of(replicas, shard % 2)[stage]
            pairs.append((replica * shards + shard, other * shards + shard))
    return lax.ppermute(value, ("replica", "shard"), pairs)


def tied(values, *others):
    leaves, tree = jax.tree.flatten(values)
    held = lax.optimization_barrier((*leaves, *jax.tree.leaves(others)))
    return jax.tree.unflatten(tree, held[: len(leaves)])


def dot(left, right):
    return jnp.dot(left, right, preferred_element_type=F32)


def dot_tb(left, right):
    return lax.dot_general(left, right, (((1,), (1,)), ((), ())), preferred_element_type=F32)


def dot_ta(left, right):
    return lax.dot_general(left, right, (((0,), (0,)), ((), ())), preferred_element_type=F32)


def chunk_index(me, size, skip):
    orders = [xor_order(stages_of(size, core)[skip:]) for core in (0, 1)]
    return [jnp.where(me % 2 == 0, one, other) for one, other in zip(*orders, strict=True)]


def first_bit(me, size):
    return jnp.where(me % 2 == 0, stages_of(size, 0)[0], stages_of(size, 1)[0])


def normalized(values):
    center = values - jnp.mean(values, axis=-1, keepdims=True)
    spread = jnp.mean(center * center, axis=-1, keepdims=True)
    root = lax.rsqrt(spread + 1e-05)
    return center * root, root


def pack_kernel(slots, *refs):
    count = len(PACKED)
    sources, (dy, near, expand_y, expand_d, joined_y, joined_d), targets = (
        refs[:count], refs[count : count + 6], refs[count + 6 : 2 * count + 6]
    )
    sems = refs[-1]
    copies = [pltpu.make_async_copy(*pair, sems.at[i]) for i, pair in enumerate(zip(sources, targets, strict=True))]
    for copy in copies:
        copy.start()
    for copy in copies:
        copy.wait()
    joined, expand, cot, seg, pad, joined_bias, *gain_refs = targets
    me, column = lax.axis_index("shard"), lax.axis_index("replica") % 2
    rows = []
    for s in range(2):
        live = pad[s : s + 1, :] * slots[0, s]
        code = jnp.where(live > 0, seg[s : s + 1, :], -1).astype(F32)
        rows.append((seg[s : s + 1, :].astype(F32), code))
        alive = jnp.transpose(jnp.broadcast_to(live.astype(F32), (8, 128)))[:, 0:1]
        dy[s * 128 : (s + 1) * 128, :] = jnp.where(alive > 0.0, cot[s].astype(F32), 0.0).astype(BF16)
    docs = jnp.concatenate([rows[0][0], rows[1][0], rows[0][1], rows[1][1]], axis=1)
    gains = jnp.concatenate([ref[...].astype(F32).reshape(1, 128) for ref in gain_refs], axis=1)
    bias = jnp.concatenate([joined_bias[...].astype(F32).reshape(1, 384), jnp.zeros((1, 128), F32)], axis=1)
    dy[256:, :] = jnp.concatenate([docs, gains, bias, jnp.zeros((META - 3, D), F32)], axis=0).astype(BF16)
    half = pl.ds(pl.multiple_of(column * 64, 64), 64)
    expand_y[...] = expand[half, pl.ds(pl.multiple_of((me ^ 2) * 512, 512), 512)]
    expand_d[...] = expand[half, pl.ds(pl.multiple_of((me ^ 3) * 512, 512), 512)]
    near[0] = expand[:, pl.ds(pl.multiple_of((me ^ 1) * 512, 512), 512)]
    copy_joined(joined, me ^ 1, near.at[1])
    near[1, :, 384:512] = jnp.zeros((128, 128), BF16)
    copy_joined(joined, me ^ 2, joined_y)
    copy_joined(joined, me ^ 3, joined_d)


def copy_kernel(source, target):
    target[...] = source[...]


def copy_joined(joined, j, target):
    for third in range(3):
        start = pl.multiple_of(third * D + j * 128, 128)
        target[0:128, third * 128 : (third + 1) * 128] = joined[:, pl.ds(start, 128)]


def meta_row(meta_s, line, start, stop):
    return jnp.concatenate([meta_s[j, line : line + 1, start:stop] for j in range(4)], axis=1)


def mlp_kernel(
    t0, t1, t2, t3, d0, d1, d2, d3, expand, near, expand_y, expand_d, expand_x, shrink, bias,
    act_s, inner_s, expand_s, vec_out, meta_s, *rest, split,
):
    outs, (second_s, dy_s, grad_s) = rest[:-3], rest[-3:]
    me, mine = lax.axis_index("shard"), lax.axis_index("replica")
    column = mine % 2
    for k, cot in enumerate((d0, d1, d2, d3)):
        meta_s[me ^ k] = cot[256:, :].astype(F32)

    def rows_of(k, start, size):
        return pl.ds(pl.multiple_of((me ^ k) * 128 + start, 64), size)

    expand_s[rows_of(0, 0, 128), :] = expand[:, pl.ds(pl.multiple_of(me * 512, 512), 512)]
    expand_s[rows_of(1, 0, 128), :] = near[0]
    for k, straight in ((2, expand_y), (3, expand_d)):
        expand_s[rows_of(k, column * 64, 64), :] = straight[...]
        expand_s[rows_of(k, (1 - column) * 64, 64), :] = expand_x[k - 2]
    gain = meta_row(meta_s, 1, 256, 384)
    shift = meta_row(meta_s, 1, 384, 512)
    vec_bias = jnp.zeros((1, 512), F32)
    vec_dy = jnp.zeros((1, D), F32)
    for k, (tok, cot) in enumerate(((t0, d0), (t1, d1), (t2, d2), (t3, d3))):
        rows = slice(k * 256, (k + 1) * 256)
        hat, _ = normalized(tok[...].astype(F32))
        second = (hat * gain + shift).astype(BF16)
        second_s[rows, :] = second
        inner = dot(second, expand_s[...]) + bias[...]
        half = 0.5 + 0.5 * lax.erf(inner * (0.5**0.5))
        act = (inner * half).astype(BF16)
        act_s[rows, :] = act
        slope = half + inner * jnp.exp(inner * inner * -0.5) * ((0.5 / np.pi) ** 0.5)
        dy = cot[0:256, :]
        dy_s[rows, :] = dy
        d_inner = (dot_tb(dy, shrink[...]) * slope).astype(BF16)
        inner_s[rows, :] = d_inner
        vec_bias += jnp.sum(d_inner.astype(F32), axis=0, keepdims=True)
        vec_dy += jnp.sum(dy.astype(F32), axis=0, keepdims=True)
    vec_out[...] = jnp.zeros_like(vec_out)
    vec_out[5:6, :] = vec_bias
    vec_out[6:7, :] = vec_dy
    grad_shrink = dot_ta(act_s[...], dy_s[...]).astype(BF16)
    grad_expand = dot_ta(second_s[...], inner_s[...]).astype(BF16)
    if not split:
        outs[0][0] = grad_shrink
        outs[0][1] = grad_expand
        return
    part = 128 // split
    grad_s[:, 0:4] = grad_shrink.reshape(split, 4, part, D)
    for j in range(4):
        grad_s[:, 4 + (me ^ j)] = grad_expand[j * 128 : (j + 1) * 128].reshape(split, part, D)
    for i, c in enumerate(chunk_index(me, split, 1)):
        outs[0][i] = grad_s[mine ^ c].reshape(8 * part, D)
        outs[1][i] = grad_s[mine ^ c ^ first_bit(me, split)].reshape(8 * part, D)


def turned(values, cosine, sine_up, sine_down, sign):
    up = pltpu.roll(values, 120, 1)
    down = pltpu.roll(values, 8, 1)
    return values * cosine + (up * sine_up + down * sine_down) * sign


def attention_kernel(
    t0, t1, t2, t3, d0, d1, d2, d3, meta_s, dense, dense_bias, shrink_bias, table, act, inner, expand_w, shrink, vec_in,
    *rest, slot, split,
):
    s = slot
    if s == 0:
        (joined, near, joined_y, joined_d), rest = rest[:4], rest[4:]
        (keep_out, send_out, joined_out, dense_out, vec_out, joined_w), rest = rest[:6], rest[6:]
    else:
        (joined_in, dense_in, joined_w), rest = rest[:3], rest[3:]
        (keep_out, send_out), rest = rest[:2], rest[2:]
    outs, (bias_s, tok_s, dy_s, act_s, inner_s, both_s, grad_s) = rest[:-7], rest[-7:]
    if s == 0:
        me = lax.axis_index("shard")
        copy_joined(joined, me, joined_w.at[pl.ds(pl.multiple_of(me * 128, 128), 128)])
        for k, block in ((1, near.at[1]), (2, joined_y), (3, joined_d)):
            joined_w[pl.ds(pl.multiple_of((me ^ k) * 128, 128), 128), :] = block[:, 0:384]
    me, mine = lax.axis_index("shard"), lax.axis_index("replica")
    for k, (tok, cot) in enumerate(((t0, d0), (t1, d1), (t2, d2), (t3, d3))):
        start = pl.multiple_of((me ^ k) * 128, 128)
        tok_s[pl.ds(start, 128), :] = tok[s * 128 : (s + 1) * 128, :]
        dy_s[pl.ds(start, 128), :] = cot[s * 128 : (s + 1) * 128, :]
        rows = slice(k * 256 + s * 128, k * 256 + (s + 1) * 128)
        act_s[pl.ds(start, 128), :] = act[rows, :]
        inner_s[pl.ds(start, 128), :] = inner[rows, :]
    gain = meta_row(meta_s, 1, 0, 128)
    shift = meta_row(meta_s, 1, 128, 256)
    bias_s[0:1, :] = meta_row(meta_s, 2, 0, 384)
    joined_bias = jnp.concatenate(
        [bias_s[0:1, pl.ds(pl.multiple_of(part * D + me * 128, 128), 128)] for part in range(3)], axis=1
    )
    low_half = lax.broadcasted_iota(jnp.int32, (1, 128), 1) < HEAD_DIM
    cosine = table[:, 0:128]
    sine_up = table[:, 128:256]
    sine_down = table[:, 256:384]
    zero = jnp.zeros((), BF16)
    hat, _ = normalized(tok_s[...].astype(F32))
    first = (hat * gain + shift).astype(BF16)
    joined = dot(first, joined_w[...]) + joined_bias
    query = (turned(joined[:, 0:128], cosine, sine_up, sine_down, 1.0) * (HEAD_DIM**-0.5)).astype(BF16)
    key = turned(joined[:, 128:256], cosine, sine_up, sine_down, 1.0).astype(BF16)
    value = joined[:, 256:384].astype(BF16)
    dy = dy_s[...]
    d_heads = dot_tb(dy, dense[...]).astype(BF16)
    query_doc = jnp.transpose(
        jnp.broadcast_to(meta_row(meta_s, 0, s * 128, (s + 1) * 128), (8, 512))
    )[:, 0:1]
    key_doc = meta_row(meta_s, 0, 256 + s * 128, 256 + (s + 1) * 128)
    query_grads = []
    heads_parts = []
    key_grad = jnp.zeros((128, 512), F32)
    value_grad = jnp.zeros((128, 512), F32)
    for block in range(2):
        lo, hi = block * 256, (block + 1) * 256
        at = lax.broadcasted_iota(jnp.int32, (256, hi), 0) + lo
        to = lax.broadcasted_iota(jnp.int32, (256, hi), 1)
        allowed = ((query_doc[lo:hi] == key_doc[:, :hi]) & (to <= at)) | (to == at)
        out = jnp.zeros((256, 128), F32)
        query_grad = jnp.zeros((256, 128), F32)
        key_part = jnp.zeros((128, hi), F32)
        value_part = jnp.zeros((128, hi), F32)
        for h in range(2):
            ours = low_half if h == 0 else jnp.logical_not(low_half)
            q_h = jnp.where(ours, query[lo:hi], zero)
            k_h = jnp.where(ours, key[:hi], zero)
            v_h = jnp.where(ours, value[:hi], zero)
            g_h = jnp.where(ours, d_heads[lo:hi], zero)
            scores = jnp.where(allowed, dot_tb(q_h, k_h), -1e30)
            top = jnp.max(scores, axis=-1, keepdims=True)
            expd = jnp.exp(scores - top)
            probs = expd * (1.0 / jnp.sum(expd, axis=-1, keepdims=True))
            probs_low = probs.astype(BF16)
            out += dot(probs_low, v_h)
            d_probs = dot_tb(g_h, v_h)
            weighted = d_probs * probs
            d_scores = (weighted - probs * jnp.sum(weighted, axis=-1, keepdims=True)).astype(BF16)
            query_grad += dot(d_scores, k_h)
            key_part += dot_ta(q_h, d_scores)
            value_part += dot_ta(g_h, probs_low)
        query_grads.append(query_grad)
        heads_parts.append(out)
        if hi < 512:
            pad = jnp.zeros((128, 512 - hi), F32)
            key_part = jnp.concatenate([key_part, pad], axis=1)
            value_part = jnp.concatenate([value_part, pad], axis=1)
        key_grad += key_part
        value_grad += value_part
    heads = jnp.concatenate(heads_parts, axis=0).astype(BF16)
    query_grad = jnp.concatenate(query_grads, axis=0) * (HEAD_DIM**-0.5)
    d_joined = jnp.concatenate(
        [
            turned(query_grad, cosine, sine_up, sine_down, -1.0),
            turned(jnp.transpose(key_grad), cosine, sine_up, sine_down, -1.0),
            jnp.transpose(value_grad),
        ],
        axis=1,
    ).astype(BF16)
    d_first = dot_tb(d_joined, joined_w[...])
    d_second = dot_tb(inner_s[...], expand_w[...])
    grad_in = d_first * gain + d_second * meta_row(meta_s, 1, 256, 384)
    own_columns = lax.broadcasted_iota(jnp.int32, (1, D), 1) // 128 == me
    out_bias = dense_bias[...] + shrink_bias[...]
    branches = dot(heads, dense[...]) + dot(act_s[...], shrink[...]) + jnp.where(own_columns, jnp.concatenate([out_bias] * 4, axis=1), 0.0)
    for j in range(4):
        piece = slice(j * 128, (j + 1) * 128)
        both_s[j, 0] = branches[piece].astype(BF16)
        both_s[j, 1] = grad_in[piece].astype(BF16)
    for i in range(2):
        keep_out[i] = both_s[me ^ (2 * i)]
        send_out[i] = both_s[me ^ (2 * i + 1)]
    grad_joined = dot_ta(first, d_joined)
    grad_dense = dot_ta(heads, dy)
    vec = vec_in[...]
    line = lax.broadcasted_iota(jnp.int32, (8, D), 0)
    vec = vec + jnp.where(line == 0, jnp.sum(d_first * hat, axis=0, keepdims=True), 0.0)
    vec = vec + jnp.where(line == 1, jnp.sum(d_first, axis=0, keepdims=True), 0.0)
    vec = vec + jnp.where(line == 2, jnp.sum(d_second * hat, axis=0, keepdims=True), 0.0)
    vec = vec + jnp.where(line == 3, jnp.sum(d_second, axis=0, keepdims=True), 0.0)
    bias_line = jnp.concatenate(
        [jnp.sum(d_joined.astype(F32), axis=0, keepdims=True), jnp.zeros((1, 128), F32)], axis=1
    )
    vec = vec + jnp.where(line == 4, bias_line, 0.0)
    if s == 0:
        joined_out[...] = grad_joined
        dense_out[...] = grad_dense
        vec_out[...] = vec
        return
    grad_joined = (grad_joined + joined_in[...]).astype(BF16)
    grad_dense = (grad_dense + dense_in[...]).astype(BF16)
    if not split:
        for j in range(4):
            outs[0][j, :, 0:384] = grad_joined[j * 128 : (j + 1) * 128]
            outs[0][j, :, 384:512] = grad_dense[:, j * 128 : (j + 1) * 128]
        outs[1][...] = vec
        return
    part = 128 // split
    for j in range(4):
        for third in range(3):
            block = grad_joined[j * 128 : (j + 1) * 128, third * 128 : (third + 1) * 128]
            grad_s[:, 4 * (me ^ j) + third] = block.reshape(split, part, 128)
        grad_s[:, 4 * j + 3] = grad_dense[:, j * 128 : (j + 1) * 128].reshape(split, part, 128)
    for r in range(split):
        quarters = [vec[r % 8 : r % 8 + 1, q * 128 : (q + 1) * 128] for q in range(4)]
        grad_s[r, 16] = jnp.concatenate(quarters + [jnp.zeros((LINES - 4, 128), F32)], axis=0).astype(BF16)
    for i, c in enumerate(chunk_index(me, split, 1)):
        outs[0][i] = grad_s[mine ^ c].reshape(16 * part + LINES, 128)
        outs[1][i] = grad_s[mine ^ c ^ first_bit(me, split)].reshape(16 * part + LINES, 128)


def rows_kernel(keep0, keep1, near0, near1, own, send):
    for slot, (keep, near) in enumerate(((keep0, near0), (keep1, near1))):
        own[slot] = keep[0].astype(F32) + near[0].astype(F32)
        send[slot] = (keep[1].astype(F32) + near[1].astype(F32)).astype(BF16)


def fold_kernel(keep, arrived, kept, send):
    half = kept.shape[0]
    for i in range(half):
        kept[i] = keep[i].astype(F32) + arrived[i].astype(F32)
        send[i] = (keep[half + i].astype(F32) + arrived[half + i].astype(F32)).astype(BF16)


def fold_last_kernel(keep, arrived, total):
    total[...] = (keep[...].astype(F32) + arrived[...].astype(F32)).astype(BF16)


def concat_kernel(held, arrived, out):
    size = held.shape[0]
    out[0:size] = held[...]
    out[size:] = arrived[...]


def mlp_cut_kernel(pair, arrived, own, *sends, part):
    for c in range(2):
        own[c] = (pair[c].astype(F32) + arrived[1 - c].astype(F32)).astype(BF16)
        for k in (1, 2, 3):
            sends[k - 1][c * part : (c + 1) * part, :] = own[c, (4 + k) * part : (5 + k) * part, :]


def mlp_arrange_kernel(own, near, across, diagonal, held, *, part):
    for c in range(2):
        held[c, : 5 * part] = own[c, : 5 * part, :]
        for k, item in ((1, near), (2, across), (3, diagonal)):
            held[c, (4 + k) * part : (5 + k) * part] = item[c * part : (c + 1) * part, :]


def attention_cut_kernel(pair, arrived, own, *sends, part):
    for c in range(2):
        own[c] = (pair[c].astype(F32) + arrived[1 - c].astype(F32)).astype(BF16)
    lines = jnp.concatenate(
        [own[c, 16 * part :, :].astype(F32)[0:4] for c in range(2)] + [jnp.zeros((LINES - 8, 128), F32)], axis=0
    ).astype(BF16)
    for k in (1, 2, 3):
        for c in range(2):
            sends[k - 1][c * 3 * part : (c + 1) * 3 * part, :] = own[c, 4 * k * part : (4 * k + 3) * part, :]
        sends[k - 1][6 * part :, :] = lines


def attention_arrange_kernel(own, near, across, diagonal, held, *, part):
    for c in range(2):
        lines = [own[c, 16 * part :, :].astype(F32)[0:4]]
        held[c, 0 : 3 * part] = own[c, 0 : 3 * part, :]
        for k, item in ((1, near), (2, across), (3, diagonal)):
            held[c, 4 * k * part : (4 * k + 3) * part] = item[c * 3 * part : (c + 1) * 3 * part, :]
            lines.append(item[6 * part :, :].astype(F32)[4 * c : 4 * c + 4])
        for k in range(4):
            held[c, (4 * k + 3) * part : (4 * k + 4) * part] = own[c, (4 * k + 3) * part : (4 * k + 4) * part, :]
        held[c, 16 * part :] = jnp.concatenate(lines, axis=0).astype(BF16)


def finish_kernel(keep, arrived, tok, cot, out, grad):
    for slot in range(2):
        tokens = tok[slot].astype(F32)
        out[slot] = (tokens + keep[slot, 0] + arrived[slot, 0].astype(F32)).astype(BF16)
        e = keep[slot, 1] + arrived[slot, 1].astype(F32)
        hat, root = normalized(tokens)
        mean_e = jnp.mean(e, axis=-1, keepdims=True)
        mean_eh = jnp.mean(e * hat, axis=-1, keepdims=True)
        grad[slot] = cot[slot * 128 : (slot + 1) * 128, :].astype(F32) + root * (e - mean_e - hat * mean_eh)


def mlp_place_kernel(held, arrived, shrink_out, expand_out, *, split):
    me, mine = lax.axis_index("shard"), lax.axis_index("replica")
    part = 128 // split
    half = split // 2
    for i, c in enumerate(chunk_index(me, split, 0)):
        block = (held if i < half else arrived)[i % half].astype(F32)
        shrink_out[pl.ds(pl.multiple_of((mine ^ c) * 4 * part, 4 * part), 4 * part), :] = block[: 4 * part]
        rows = pl.ds(pl.multiple_of((mine ^ c) * part, part), part)
        for k in range(4):
            columns = pl.ds(pl.multiple_of((me ^ k) * 512, 512), 512)
            expand_out[rows, columns] = block[(4 + k) * part : (5 + k) * part]


def attention_place_kernel(
    held, arrived, joined_out, dense_out, bias_out, dense_bias_out, expand_bias_out, shrink_bias_out,
    gain1_out, shift1_out, gain2_out, shift2_out, vec_s, bias_s, *, split,
):
    me, mine = lax.axis_index("shard"), lax.axis_index("replica")
    part = 128 // split
    half = split // 2
    for i, c in enumerate(chunk_index(me, split, 0)):
        block = (held if i < half else arrived)[i % half].astype(F32)
        r = mine ^ c
        rows = pl.ds(pl.multiple_of(r * part, part), part)
        for k in range(4):
            tiles = [block[(4 * k + t) * part : (4 * k + t + 1) * part] for t in range(4)]
            for third in range(3):
                columns = pl.ds(pl.multiple_of(third * D + (me ^ k) * 128, 128), 128)
                joined_out[rows, columns] = tiles[third]
            dense_out[rows, k * 128 : (k + 1) * 128] = tiles[3]
        vec_s[r] = block[16 * part :]

    row = lax.broadcasted_iota(jnp.int32, (LINES, 128), 0)
    for line, target in ((0, gain1_out), (1, shift1_out), (2, gain2_out), (3, shift2_out)):
        target[...] = jnp.sum(jnp.where(row % 4 == me, vec_s[line], 0.0), axis=0)
    dense_line = jnp.sum(jnp.where(row == me, vec_s[6], 0.0), axis=0)
    dense_bias_out[...] = dense_line
    shrink_bias_out[...] = dense_line
    for k in range(4):
        for third in range(3):
            columns = pl.ds(pl.multiple_of(third * D + (me ^ k) * 128, 128), 128)
            bias_s[0:1, columns] = vec_s[4, 4 * k + third : 4 * k + third + 1]
    bias_out[...] = bias_s[0:1, pl.ds(pl.multiple_of(me * 384, 128), 384)].reshape(384)
    expand_bias_out[...] = jnp.concatenate([vec_s[5, q : q + 1] for q in range(4)], axis=1).reshape(512)


def rope_table(length):
    half = ROT // 2
    freqs = (10000.0 ** (-2.0 * np.arange(half, dtype=np.float64) / ROT)).astype(np.float32)
    angles = np.arange(length, dtype=np.float32)[:, None] * freqs[None, :]
    cosine = np.ones((length, HEAD_DIM), np.float32)
    up = np.zeros((length, HEAD_DIM), np.float32)
    down = np.zeros((length, HEAD_DIM), np.float32)
    cosine[:, :half] = np.cos(angles)
    cosine[:, half:ROT] = np.cos(angles)
    up[:, :half] = -np.sin(angles)
    down[:, half:ROT] = np.sin(angles)
    return np.concatenate([np.tile(part, (1, 2)) for part in (cosine, up, down)], axis=1)


def per_device(
    tokens,
    cotangent,
    segments,
    pad_mask,
    slot_table,
    joined_weight,
    joined_bias,
    dense_weight,
    dense_bias,
    expand_weight,
    expand_bias,
    shrink_weight,
    shrink_bias,
    first_gain,
    first_shift,
    second_gain,
    second_shift,
):
    replicas = lax.axis_size("replica")
    me = lax.axis_index("shard")
    mine = lax.axis_index("replica")
    part = 128 // replicas
    split = replicas if part % 16 == 0 and replicas >= 8 else 0
    steps = replicas.bit_length() - 1
    smem = pl.BlockSpec(memory_space=pltpu.SMEM)
    vmem = pl.BlockSpec(memory_space=pltpu.VMEM)
    shaped = jax.ShapeDtypeStruct

    def call(kernel, name, *, work, outs, scratch, args, limit=12):
        return pl.pallas_call(
            kernel,
            cost_estimate=pl.CostEstimate(flops=work, bytes_accessed=work // 300, transcendentals=0),
            out_shape=tuple(outs),
            in_specs=[vmem] * len(args),
            out_specs=(vmem,) * len(outs),
            scratch_shapes=[pltpu.VMEM(*item) for item in scratch],
            compiler_params=pltpu.CompilerParams(vmem_limit_bytes=limit * 1024 * 1024),
            name=name,
        )(*args)

    small = functools.partial(call, work=1000, scratch=[], limit=8)

    tok = tokens[0].reshape(256, D)
    tok_across = exchange(tok, "shard", 2)
    tok_near = exchange(tok, "shard", 1)
    half_block, joined_block = shaped((64, D), BF16), shaped((128, 384), BF16)
    dy, near_send, expand_y, expand_d, joined_y, joined_d = pl.pallas_call(
        pack_kernel,
        cost_estimate=pl.CostEstimate(flops=2 * 10**9, bytes_accessed=6 * 10**6, transcendentals=0),
        out_shape=(
            shaped((256 + META, D), BF16), shaped((2, 128, D), BF16), half_block, half_block, joined_block, joined_block
        ),
        in_specs=[smem] + [pl.BlockSpec(memory_space=pltpu.HBM)] * len(PACKED),
        out_specs=(vmem,) * 6,
        scratch_shapes=[pltpu.VMEM(*item) for item in PACKED] + [pltpu.SemaphoreType.DMA((len(PACKED),))],
        compiler_params=pltpu.CompilerParams(vmem_limit_bytes=60 * 1024 * 1024),
        name="pack_weights",
    )(
        slot_table, joined_weight, expand_weight, cotangent[0], segments[0], pad_mask[0], joined_bias,
        first_gain, first_shift, second_gain, second_shift,
    )
    near = exchange(near_send, "shard", 1)
    expand_y = exchange(expand_y, "shard", 2)
    expand_d = exchange(expand_d, "shard", 3)
    dy_near = exchange(dy, "shard", 1)
    dy_across = exchange(tied(dy, expand_y, expand_d, tok_across), "shard", 2)
    tok_far = exchange(tok_across, "shard", 1)
    (dy_own,) = small(copy_kernel, "hold_rows", outs=[shaped(dy.shape, BF16)], args=(dy,))
    expand_x = exchange(tied(jnp.stack([expand_y, expand_d]), dy_own, tok_across), "replica", 1)
    held = tied((dy_across, joined_y, joined_d, expand_x, near, dy_near, tok_near, tok_far))
    dy_across, joined_y, joined_d, expand_x, near, dy_near, tok_near, tok_far = held
    joined_y = exchange(joined_y, "shard", 2)
    joined_d = exchange(joined_d, "shard", 3)
    dy_far = exchange(dy_across, "shard", 1)
    toks = (tok, tok_near, tok_across, tok_far)
    dys = (dy_own, dy_near, dy_across, dy_far)

    xor4 = me ^ jnp.arange(4, dtype=jnp.int32)
    order = jnp.where(me % 2 == 0, *[jnp.asarray(xor_order(stages_of(replicas, core)), jnp.int32) for core in (0, 1)])

    def halves(chunks):
        ordered = chunks[mine ^ order]
        return [ordered[: replicas // 2], ordered[replicas // 2 :]]

    def by_owner(pair):
        place_of = jnp.zeros((replicas,), jnp.int32).at[mine ^ order].set(jnp.arange(replicas, dtype=jnp.int32))
        return jnp.concatenate(pair, axis=0)[place_of].astype(F32)

    rows1024 = shaped((1024, 512), BF16)
    vec_shape = shaped((8, D), F32)
    act, inner, expand_all, vec_mlp, meta_all, *mlp_state = call(
        functools.partial(mlp_kernel, split=split),
        "mlp_branch",
        work=4 * 10**9,
        outs=[rows1024, rows1024, shaped((512, 512), BF16), vec_shape, shaped((4, META, D), F32)]
        + ([shaped((replicas // 2, 8 * part, D), BF16)] * 2 if split else [shaped((2, 512, D), BF16)]),
        scratch=[
            ((1024, D), BF16),
            ((1024, D), BF16),
            ((8, 8, 16, D), BF16),
        ],
        args=(*toks, *dys, expand_weight, near, expand_y, expand_d, expand_x, shrink_weight, expand_bias.astype(F32).reshape(1, 512)),
    )
    if not split:
        blocks = mlp_state[0][1].reshape(4, replicas, part, D).transpose(1, 0, 2, 3)[:, xor4]
        mlp_state = halves(
            jnp.concatenate(
                [mlp_state[0][0].reshape(replicas, 4 * part, D), blocks.reshape(replicas, 4 * part, D)], axis=1
            )
        )
    def folded(keep, arrived, last=False, work=1000):
        chunks = keep.shape
        half = shaped((chunks[0] // 2, *chunks[1:]), F32), shaped((chunks[0] // 2, *chunks[1:]), BF16)
        if split and last:
            outs = [shaped(chunks, BF16)]
            return call(fold_last_kernel, "fold", work=work, outs=outs, scratch=[], args=(keep, arrived), limit=8)[0]
        if split:
            return small(fold_kernel, "fold", outs=half, args=(keep, arrived))
        total = keep.astype(F32) + arrived.astype(F32)
        if last:
            return total.astype(BF16)
        return total[: chunks[0] // 2], total[chunks[0] // 2 :].astype(BF16)

    def middle(pair):
        return replica_exchange(pair, steps - 1)

    def doubled(held, arrived, work=1000):
        if split:
            whole = shaped((2 * held.shape[0], *held.shape[1:]), BF16)
            return call(concat_kernel, "double", work=work, outs=[whole], scratch=[], args=(held, arrived), limit=8)[0]
        return jnp.concatenate([held, arrived], axis=0)

    def to_owners(sends):
        return [exchange(send, "shard", k) for k, send in zip((1, 2, 3), sends, strict=True)]

    mlp_state = folded(mlp_state[0], replica_exchange(mlp_state[1], 0))

    half_rows = shaped((2, 2, 128, D), BF16)
    scratch = [
        ((8, 3 * D), F32),
        ((512, D), BF16),
        ((512, D), BF16),
        ((512, 512), BF16),
        ((512, 512), BF16),
        ((4, 2, 128, D), BF16),
        ((8, 17, 16, 128), BF16),
    ]
    common = (
        *toks, *dys, meta_all, dense_weight,
        dense_bias.astype(F32).reshape(1, 128), shrink_bias.astype(F32).reshape(1, 128),
        rope_table(4 * 128), act, inner, expand_all, shrink_weight,
    )
    keep0, send0, joined_part, dense_part, vec_part, joined_all = call(
        functools.partial(attention_kernel, slot=0, split=split),
        "attention_first_slot",
        work=6 * 10**9,
        outs=[half_rows, half_rows, shaped((512, 384), F32), shaped((128, D), F32), vec_shape, shaped((512, 384), BF16)],
        scratch=scratch,
        args=(*common, vec_mlp, joined_weight, near, joined_y, joined_d),
    )
    keep1, send1, *att_state = call(
        functools.partial(attention_kernel, slot=1, split=split),
        "attention_second_slot",
        work=6 * 10**9,
        outs=[half_rows, half_rows]
        + ([shaped((replicas // 2, 16 * part + LINES, 128), BF16)] * 2 if split else [shaped((4, 128, D), BF16), vec_shape]),
        scratch=scratch,
        args=(*common, tied(vec_part, mlp_state[1]), joined_part, dense_part, joined_all),
    )
    if not split:
        blocks = att_state[0].reshape(4, replicas, part, 4, 128).transpose(1, 0, 3, 2, 4)
        blocks = jnp.concatenate([blocks[:, xor4][:, :, :3], blocks[:, :, 3:]], axis=2).reshape(replicas, 16 * part, 128)
        line = jnp.pad(att_state[1].reshape(8, 4, 128), ((0, replicas - 8), (0, LINES - 4), (0, 0))).astype(BF16)
        att_state = halves(jnp.concatenate([blocks, line], axis=1))

    for stage in range(1, steps - 1):
        mlp_state = folded(mlp_state[0], replica_exchange(mlp_state[1], stage), stage == steps - 2)

    mlp_pair = mlp_state
    att_state = folded(att_state[0], replica_exchange(tied(att_state[1], mlp_pair), 0))
    from_near = [exchange(tied(send, att_state), "shard", 1) for send in (send0, send1)]
    rows_own, rows_send = small(
        rows_kernel,
        "rows_between_cores",
        outs=[shaped((2, 2, 128, D), F32), shaped((2, 2, 128, D), BF16)],
        args=(keep0, keep1, *from_near),
    )
    rows_arrived = exchange(rows_send, "shard", 2)

    arrived, mlp_new = tied((replica_exchange(att_state[1], 1), middle(mlp_pair)))
    att_pair = folded(att_state[0], arrived, steps == 3, 2 * 10**10)
    for stage in range(2, steps - 1):
        att_pair = folded(att_pair[0], replica_exchange(att_pair[1], stage), stage == steps - 2)
    if split:
        mlp_own, *mlp_sends = small(
            functools.partial(mlp_cut_kernel, part=part),
            "cut_mlp_grads",
            outs=[shaped((2, 8 * part, D), BF16)] + [shaped((2 * part, D), BF16)] * 3,
            args=(mlp_pair, mlp_new),
        )
    else:
        mlp_own = (mlp_pair.astype(F32) + mlp_new[::-1].astype(F32)).astype(BF16)
        mlp_sends = [mlp_own[:, (4 + k) * part : (5 + k) * part].reshape(2 * part, D) for k in (1, 2, 3)]
    att_new, moved = tied((middle(att_pair), to_owners(mlp_sends)))
    if split:
        (mlp_held,) = small(
            functools.partial(mlp_arrange_kernel, part=part),
            "arrange_mlp_grads",
            outs=[shaped((2, 8 * part, D), BF16)],
            args=(mlp_own, *moved),
        )
    else:
        mlp_held = jnp.concatenate([mlp_own[:, : 5 * part], *[item.reshape(2, part, D) for item in moved]], axis=1)

    if split:
        att_own, *att_sends = small(
            functools.partial(attention_cut_kernel, part=part),
            "cut_attention_grads",
            outs=[shaped((2, 16 * part + LINES, 128), BF16)] + [shaped((6 * part + LINES, 128), BF16)] * 3,
            args=(att_pair, att_new),
        )
    else:
        att_own = (att_pair.astype(F32) + att_new[::-1].astype(F32)).astype(BF16)
        lines = att_own[:, 16 * part : 16 * part + 4].reshape(8, 128)
        att_sends = [
            jnp.concatenate([att_own[:, 4 * k * part : (4 * k + 3) * part].reshape(6 * part, 128), lines], axis=0)
            for k in (1, 2, 3)
        ]
    moved = to_owners(att_sends)
    if split:
        (att_held,) = call(
            functools.partial(attention_arrange_kernel, part=part),
            "arrange_attention_grads",
            work=2 * 10**10,
            scratch=[],
            outs=[shaped((2, 16 * part + LINES, 128), BF16)],
            args=(att_own, *moved),
        )
    else:
        pieces, lines = [att_own[:, : 4 * part]], [att_own[:, 16 * part : 16 * part + 4]]
        for k, item in zip((1, 2, 3), moved):
            pieces += [item[: 6 * part].reshape(2, 3 * part, 128), att_own[:, (4 * k + 3) * part : (4 * k + 4) * part]]
            lines.append(item[6 * part :].reshape(2, 4, 128))
        att_held = jnp.concatenate([*pieces, *lines], axis=1)

    for stage in reversed(range(1, steps - 1)):
        mlp_held = doubled(mlp_held, tied(replica_exchange(mlp_held, stage), att_held))
        att_held = doubled(att_held, replica_exchange(att_held, stage), 2 * 10**10)
    mlp_done = mlp_held, replica_exchange(mlp_held, 0)
    att_done = att_held, replica_exchange(att_held, 0)

    def finish(rows_new):
        return small(
            finish_kernel,
            "finish_rows",
            outs=[shaped((2, 128, D), BF16), shaped((2, 128, D), F32)],
            args=(rows_own, rows_new, tokens[0], dy_own),
        )

    if split:
        grad_shrink, grad_expand = small(
            functools.partial(mlp_place_kernel, split=split),
            "place_mlp_grads",
            outs=[shaped((512, D), F32), shaped((128, FF), F32)],
            args=mlp_done,
        )
        output, input_grad = finish(tied(rows_arrived, grad_shrink))
        widths = [384, 128, 512, 128, 128, 128, 128, 128]
        grad_joined, grad_dense, *vectors = call(
            functools.partial(attention_place_kernel, split=split),
            "place_attention_grads",
            work=1000,
            outs=[shaped((128, 3 * D), F32), shaped((128, D), F32)] + [shaped((width,), F32) for width in widths],
            scratch=[((8, LINES, 128), F32), ((8, 3 * D), F32)],
            args=(att_done[0], tied(att_done[1], grad_shrink, output)),
            limit=8,
        )
    else:
        output, input_grad = finish(rows_arrived)
        mlp_all, att_all = by_owner(mlp_done), by_owner(att_done)
        grad_shrink = mlp_all[:, : 4 * part].reshape(512, D)
        blocks = mlp_all[:, 4 * part :].reshape(replicas, 4, part, D)[:, xor4]
        grad_expand = blocks.transpose(0, 2, 1, 3).reshape(128, FF)
        blocks = att_all[:, : 16 * part].reshape(replicas, 4, 4, part, 128)
        grad_dense = blocks[:, :, 3].transpose(0, 2, 1, 3).reshape(128, D)
        grad_joined = blocks[:, xor4, :3].transpose(0, 3, 2, 1, 4).reshape(128, 3 * D)
        lines = att_all[:8, 16 * part :].reshape(8, 4, D)[:, xor4]
        summed = lax.dynamic_slice_in_dim(lines[:4].sum(axis=1), me * 128, 128, axis=1)
        bias_line = lines[4, :, :384].reshape(4, 3, 128).transpose(1, 0, 2).reshape(3 * D)
        dense_line = lax.dynamic_slice_in_dim(lines[6, me], me * 128, 128, axis=0)
        vectors = [
            lax.dynamic_slice_in_dim(bias_line, me * 384, 384, axis=0),
            dense_line,
            lines[5, me],
            dense_line,
            summed[0],
            summed[1],
            summed[2],
            summed[3],
        ]
    return (
        output[None],
        input_grad[None],
        grad_joined,
        vectors[0],
        grad_dense,
        vectors[1],
        grad_expand,
        vectors[2],
        grad_shrink,
        *vectors[3:],
    )


def solution(mesh):
    rows = P("replica", None, "shard", None)
    codes = P("replica", None, "shard")
    matrix = P("shard", None)
    vector = P("shard")
    return jax.shard_map(
        per_device,
        mesh=mesh,
        in_specs=(rows, rows, codes, codes, P("replica", None))
        + (matrix, vector) * 4
        + (vector,) * 4,
        out_specs=(rows, rows) + (matrix, vector) * 4 + (vector,) * 4,
        check_vma=False,
    )
```

```python
import functools

import jax
import jax.numpy as jnp
import numpy as np
from jax import lax
from jax.experimental import pallas as pl
from jax.experimental.pallas import tpu as pltpu
from jax.sharding import PartitionSpec as P

D = 512
HEADS = 8
HEAD_DIM = 64
FF = 2048
ROT = 16
META = 16
LINES = 16
PACKED = (
    ((128, 3 * D), jnp.bfloat16),
    ((128, FF), jnp.bfloat16),
    ((2, 128, D), jnp.bfloat16),
    ((2, 128), jnp.int32),
    ((2, 128), jnp.int32),
    ((384,), jnp.bfloat16),
) + (((128,), jnp.bfloat16),) * 4

F32 = jnp.float32
BF16 = jnp.bfloat16


def exchange(value, axis, bit):
    size = lax.axis_size(axis)
    return lax.ppermute(value, axis, [(i, i ^ bit) for i in range(size)])


def xor_order(bits):
    found = [0]
    for bit in reversed(bits):
        found = found + [number | bit for number in found]
    return found


def stages_of(size, core):
    bits = [1 << place for place in range(size.bit_length() - 1)]
    return bits if core == 0 else bits[1::-1] + bits[2:]


def replica_exchange(value, stage):
    replicas, shards = lax.axis_size("replica"), lax.axis_size("shard")
    pairs = []
    for replica in range(replicas):
        for shard in range(shards):
            other = replica ^ stages_of(replicas, shard % 2)[stage]
            pairs.append((replica * shards + shard, other * shards + shard))
    return lax.ppermute(value, ("replica", "shard"), pairs)


def tied(values, *others):
    leaves, tree = jax.tree.flatten(values)
    held = lax.optimization_barrier((*leaves, *jax.tree.leaves(others)))
    return jax.tree.unflatten(tree, held[: len(leaves)])


def dot(left, right):
    return jnp.dot(left, right, preferred_element_type=F32)


def dot_tb(left, right):
    return lax.dot_general(left, right, (((1,), (1,)), ((), ())), preferred_element_type=F32)


def dot_ta(left, right):
    return lax.dot_general(left, right, (((0,), (0,)), ((), ())), preferred_element_type=F32)


def chunk_index(me, size, skip):
    orders = [xor_order(stages_of(size, core)[skip:]) for core in (0, 1)]
    return [jnp.where(me % 2 == 0, one, other) for one, other in zip(*orders, strict=True)]


def first_bit(me, size):
    return jnp.where(me % 2 == 0, stages_of(size, 0)[0], stages_of(size, 1)[0])


def normalized(values):
    center = values - jnp.mean(values, axis=-1, keepdims=True)
    spread = jnp.mean(center * center, axis=-1, keepdims=True)
    root = lax.rsqrt(spread + 1e-05)
    return center * root, root


def pack_kernel(slots, *refs):
    count = len(PACKED)
    sources, (dy, near, expand_y, expand_d, joined_y, joined_d), targets = (
        refs[:count], refs[count : count + 6], refs[count + 6 : 2 * count + 6]
    )
    sems = refs[-1]
    copies = [pltpu.make_async_copy(*pair, sems.at[i]) for i, pair in enumerate(zip(sources, targets, strict=True))]
    for copy in copies:
        copy.start()
    for copy in copies:
        copy.wait()
    joined, expand, cot, seg, pad, joined_bias, *gain_refs = targets
    me, column = lax.axis_index("shard"), lax.axis_index("replica") % 2
    rows = []
    for s in range(2):
        live = pad[s : s + 1, :] * slots[0, s]
        code = jnp.where(live > 0, seg[s : s + 1, :], -1).astype(F32)
        rows.append((seg[s : s + 1, :].astype(F32), code))
        alive = jnp.transpose(jnp.broadcast_to(live.astype(F32), (8, 128)))[:, 0:1]
        dy[s * 128 : (s + 1) * 128, :] = jnp.where(alive > 0.0, cot[s].astype(F32), 0.0).astype(BF16)
    docs = jnp.concatenate([rows[0][0], rows[1][0], rows[0][1], rows[1][1]], axis=1)
    gains = jnp.concatenate([ref[...].astype(F32).reshape(1, 128) for ref in gain_refs], axis=1)
    bias = jnp.concatenate([joined_bias[...].astype(F32).reshape(1, 384), jnp.zeros((1, 128), F32)], axis=1)
    dy[256:, :] = jnp.concatenate([docs, gains, bias, jnp.zeros((META - 3, D), F32)], axis=0).astype(BF16)
    half = pl.ds(pl.multiple_of(column * 64, 64), 64)
    expand_y[...] = expand[half, pl.ds(pl.multiple_of((me ^ 2) * 512, 512), 512)]
    expand_d[...] = expand[half, pl.ds(pl.multiple_of((me ^ 3) * 512, 512), 512)]
    near[0] = expand[:, pl.ds(pl.multiple_of((me ^ 1) * 512, 512), 512)]
    copy_joined(joined, me ^ 1, near.at[1])
    near[1, :, 384:512] = jnp.zeros((128, 128), BF16)
    copy_joined(joined, me ^ 2, joined_y)
    copy_joined(joined, me ^ 3, joined_d)


def copy_kernel(source, target):
    target[...] = source[...]


def copy_joined(joined, j, target):
    for third in range(3):
        start = pl.multiple_of(third * D + j * 128, 128)
        target[0:128, third * 128 : (third + 1) * 128] = joined[:, pl.ds(start, 128)]


def meta_row(meta_s, line, start, stop):
    return jnp.concatenate([meta_s[j, line : line + 1, start:stop] for j in range(4)], axis=1)


def mlp_kernel(
    t0, t1, t2, t3, d0, d1, d2, d3, expand, near, expand_y, expand_d, expand_x, shrink, bias,
    act_s, inner_s, expand_s, vec_out, meta_s, *rest, split,
):
    outs, (second_s, dy_s, grad_s) = rest[:-3], rest[-3:]
    me, mine = lax.axis_index("shard"), lax.axis_index("replica")
    column = mine % 2
    for k, cot in enumerate((d0, d1, d2, d3)):
        meta_s[me ^ k] = cot[256:, :].astype(F32)

    def rows_of(k, start, size):
        return pl.ds(pl.multiple_of((me ^ k) * 128 + start, 64), size)

    expand_s[rows_of(0, 0, 128), :] = expand[:, pl.ds(pl.multiple_of(me * 512, 512), 512)]
    expand_s[rows_of(1, 0, 128), :] = near[0]
    for k, straight in ((2, expand_y), (3, expand_d)):
        expand_s[rows_of(k, column * 64, 64), :] = straight[...]
        expand_s[rows_of(k, (1 - column) * 64, 64), :] = expand_x[k - 2]
    gain = meta_row(meta_s, 1, 256, 384)
    shift = meta_row(meta_s, 1, 384, 512)
    vec_bias = jnp.zeros((1, 512), F32)
    vec_dy = jnp.zeros((1, D), F32)
    for k, (tok, cot) in enumerate(((t0, d0), (t1, d1), (t2, d2), (t3, d3))):
        rows = slice(k * 256, (k + 1) * 256)
        hat, _ = normalized(tok[...].astype(F32))
        second = (hat * gain + shift).astype(BF16)
        second_s[rows, :] = second
        inner = dot(second, expand_s[...]) + bias[...]
        half = 0.5 + 0.5 * lax.erf(inner * (0.5**0.5))
        act = (inner * half).astype(BF16)
        act_s[rows, :] = act
        slope = half + inner * jnp.exp(inner * inner * -0.5) * ((0.5 / np.pi) ** 0.5)
        dy = cot[0:256, :]
        dy_s[rows, :] = dy
        d_inner = (dot_tb(dy, shrink[...]) * slope).astype(BF16)
        inner_s[rows, :] = d_inner
        vec_bias += jnp.sum(d_inner.astype(F32), axis=0, keepdims=True)
        vec_dy += jnp.sum(dy.astype(F32), axis=0, keepdims=True)
    vec_out[...] = jnp.zeros_like(vec_out)
    vec_out[5:6, :] = vec_bias
    vec_out[6:7, :] = vec_dy
    grad_shrink = dot_ta(act_s[...], dy_s[...]).astype(BF16)
    grad_expand = dot_ta(second_s[...], inner_s[...]).astype(BF16)
    if not split:
        outs[0][0] = grad_shrink
        outs[0][1] = grad_expand
        return
    part = 128 // split
    grad_s[:, 0:4] = grad_shrink.reshape(split, 4, part, D)
    for j in range(4):
        grad_s[:, 4 + (me ^ j)] = grad_expand[j * 128 : (j + 1) * 128].reshape(split, part, D)
    for i, c in enumerate(chunk_index(me, split, 1)):
        outs[0][i] = grad_s[mine ^ c].reshape(8 * part, D)
        outs[1][i] = grad_s[mine ^ c ^ first_bit(me, split)].reshape(8 * part, D)


def turned(values, cosine, sine_up, sine_down, sign):
    up = pltpu.roll(values, 120, 1)
    down = pltpu.roll(values, 8, 1)
    return values * cosine + (up * sine_up + down * sine_down) * sign


def prepared_rows(s, toks, cots, act, inner, meta_s, joined_w, joined_bias, dense, shrink, expand_w, rope, scratch):
    tok_s, dy_s, act_s, inner_s = scratch
    me = lax.axis_index("shard")
    for k, (tok, cot) in enumerate(zip(toks, cots, strict=True)):
        start = pl.multiple_of((me ^ k) * 128, 128)
        tok_s[pl.ds(start, 128), :] = tok[s * 128 : (s + 1) * 128, :]
        dy_s[pl.ds(start, 128), :] = cot[s * 128 : (s + 1) * 128, :]
        rows = slice(k * 256 + s * 128, k * 256 + (s + 1) * 128)
        act_s[pl.ds(start, 128), :] = act[rows, :]
        inner_s[pl.ds(start, 128), :] = inner[rows, :]
    hat, _ = normalized(tok_s[...].astype(F32))
    first = (hat * meta_row(meta_s, 1, 0, 128) + meta_row(meta_s, 1, 128, 256)).astype(BF16)
    joined = dot(first, joined_w[...]) + joined_bias
    query = (turned(joined[:, 0:128], *rope, 1.0) * (HEAD_DIM**-0.5)).astype(BF16)
    key = turned(joined[:, 128:256], *rope, 1.0).astype(BF16)
    value = joined[:, 256:384].astype(BF16)
    dy = dy_s[...]
    d_heads = dot_tb(dy, dense[...]).astype(BF16)
    low = jnp.concatenate([query, key, value, d_heads], axis=1)
    return hat, first, low, dy, dot(act_s[...], shrink[...]), dot_tb(inner_s[...], expand_w[...])


def attention_kernel(meta_s, dense, dense_bias, shrink_bias, table, vec_in, *rest, slot, split):
    s = slot
    me, mine = lax.axis_index("shard"), lax.axis_index("replica")
    rope = (table[:, 0:128], table[:, 128:256], table[:, 256:384])
    if s == 0:
        toks, cots, rest = rest[:4], rest[4:8], rest[8:]
        (act, inner, expand_w, shrink, joined, near, joined_y, joined_d), rest = rest[:8], rest[8:]
        (keep_out, send_out, joined_out, dense_out, vec_out, joined_w), rest = rest[:6], rest[6:]
        later, (bias_s, *rows_s, both_s) = rest[:6], rest[6:]
        copy_joined(joined, me, joined_w.at[pl.ds(pl.multiple_of(me * 128, 128), 128)])
        for k, block in ((1, near.at[1]), (2, joined_y), (3, joined_d)):
            joined_w[pl.ds(pl.multiple_of((me ^ k) * 128, 128), 128), :] = block[:, 0:384]
        bias_s[0:1, :] = meta_row(meta_s, 2, 0, 384)
        joined_bias = jnp.concatenate(
            [bias_s[0:1, pl.ds(pl.multiple_of(part * D + me * 128, 128), 128)] for part in range(3)], axis=1
        )
        given = (toks, cots, act, inner, meta_s, joined_w, joined_bias, dense, shrink, expand_w, rope, rows_s)
        for target, item in zip(later, prepared_rows(1, *given), strict=True):
            target[...] = item
        hat, first, low, dy, mlp, d_second = prepared_rows(0, *given)
    else:
        (joined_in, dense_in, joined_w), rest = rest[:3], rest[3:]
        hat, first, low, dy, mlp, d_second = [ref[...] for ref in rest[:6]]
        (keep_out, send_out), rest = rest[6:8], rest[8:]
        outs, (both_s, grad_s) = rest[:-2], rest[-2:]
    query, key, value, d_heads = [low[:, t * 128 : (t + 1) * 128] for t in range(4)]
    gain = meta_row(meta_s, 1, 0, 128)
    low_half = lax.broadcasted_iota(jnp.int32, (1, 128), 1) < HEAD_DIM
    zero = jnp.zeros((), BF16)
    query_doc = jnp.transpose(
        jnp.broadcast_to(meta_row(meta_s, 0, s * 128, (s + 1) * 128), (8, 512))
    )[:, 0:1]
    key_doc = meta_row(meta_s, 0, 256 + s * 128, 256 + (s + 1) * 128)
    both_query = jnp.concatenate([jnp.where(low_half, query, zero), jnp.where(low_half, zero, query)], axis=0)
    both_grad = jnp.concatenate([jnp.where(low_half, d_heads, zero), jnp.where(low_half, zero, d_heads)], axis=0)
    at = lax.broadcasted_iota(jnp.int32, (512, 512), 0)
    to = lax.broadcasted_iota(jnp.int32, (512, 512), 1)
    allowed = ((query_doc == key_doc) & (to <= at)) | (to == at)
    scores = dot_tb(both_query, key)
    scores = jnp.concatenate([jnp.where(allowed, scores[:512], -1e30), jnp.where(allowed, scores[512:], -1e30)], axis=0)
    expd = jnp.exp(scores - jnp.max(scores, axis=-1, keepdims=True))
    probs = expd * (1.0 / jnp.sum(expd, axis=-1, keepdims=True))
    probs_low = probs.astype(BF16)
    out = dot(probs_low, value)
    heads = jnp.where(low_half, out[:512], out[512:]).astype(BF16)
    weighted = dot_tb(both_grad, value) * probs
    d_scores = (weighted - probs * jnp.sum(weighted, axis=-1, keepdims=True)).astype(BF16)
    query_grad = dot(d_scores, key)
    query_grad = jnp.where(low_half, query_grad[:512], query_grad[512:]) * (HEAD_DIM**-0.5)
    key_grad = dot_ta(both_query, d_scores)
    value_grad = dot_ta(both_grad, probs_low)
    d_joined = jnp.concatenate(
        [
            turned(query_grad, *rope, -1.0),
            turned(jnp.transpose(key_grad), *rope, -1.0),
            jnp.transpose(value_grad),
        ],
        axis=1,
    ).astype(BF16)
    d_first = dot_tb(d_joined, joined_w[...])
    grad_in = d_first * gain + d_second * meta_row(meta_s, 1, 256, 384)
    own_columns = lax.broadcasted_iota(jnp.int32, (1, D), 1) // 128 == me
    out_bias = dense_bias[...] + shrink_bias[...]
    branches = dot(heads, dense[...]) + mlp + jnp.where(own_columns, jnp.concatenate([out_bias] * 4, axis=1), 0.0)
    for j in range(4):
        piece = slice(j * 128, (j + 1) * 128)
        both_s[j, 0] = branches[piece].astype(BF16)
        both_s[j, 1] = grad_in[piece].astype(BF16)
    for i in range(2):
        keep_out[i] = both_s[me ^ (2 * i)]
        send_out[i] = both_s[me ^ (2 * i + 1)]
    grad_joined = dot_ta(first, d_joined)
    grad_dense = dot_ta(heads, dy)
    vec = vec_in[...]
    line = lax.broadcasted_iota(jnp.int32, (8, D), 0)
    vec = vec + jnp.where(line == 0, jnp.sum(d_first * hat, axis=0, keepdims=True), 0.0)
    vec = vec + jnp.where(line == 1, jnp.sum(d_first, axis=0, keepdims=True), 0.0)
    vec = vec + jnp.where(line == 2, jnp.sum(d_second * hat, axis=0, keepdims=True), 0.0)
    vec = vec + jnp.where(line == 3, jnp.sum(d_second, axis=0, keepdims=True), 0.0)
    bias_line = jnp.concatenate(
        [jnp.sum(d_joined.astype(F32), axis=0, keepdims=True), jnp.zeros((1, 128), F32)], axis=1
    )
    vec = vec + jnp.where(line == 4, bias_line, 0.0)
    if s == 0:
        joined_out[...] = grad_joined
        dense_out[...] = grad_dense
        vec_out[...] = vec
        return
    grad_joined = (grad_joined + joined_in[...]).astype(BF16)
    grad_dense = (grad_dense + dense_in[...]).astype(BF16)
    if not split:
        for j in range(4):
            outs[0][j, :, 0:384] = grad_joined[j * 128 : (j + 1) * 128]
            outs[0][j, :, 384:512] = grad_dense[:, j * 128 : (j + 1) * 128]
        outs[1][...] = vec
        return
    part = 128 // split
    for j in range(4):
        for third in range(3):
            block = grad_joined[j * 128 : (j + 1) * 128, third * 128 : (third + 1) * 128]
            grad_s[:, 4 * (me ^ j) + third] = block.reshape(split, part, 128)
        grad_s[:, 4 * j + 3] = grad_dense[:, j * 128 : (j + 1) * 128].reshape(split, part, 128)
    for r in range(split):
        quarters = [vec[r % 8 : r % 8 + 1, q * 128 : (q + 1) * 128] for q in range(4)]
        grad_s[r, 16] = jnp.concatenate(quarters + [jnp.zeros((LINES - 4, 128), F32)], axis=0).astype(BF16)
    for i, c in enumerate(chunk_index(me, split, 1)):
        outs[0][i] = grad_s[mine ^ c].reshape(16 * part + LINES, 128)
        outs[1][i] = grad_s[mine ^ c ^ first_bit(me, split)].reshape(16 * part + LINES, 128)


def rows_kernel(keep0, keep1, near0, near1, own, send):
    for slot, (keep, near) in enumerate(((keep0, near0), (keep1, near1))):
        own[slot] = keep[0].astype(F32) + near[0].astype(F32)
        send[slot] = (keep[1].astype(F32) + near[1].astype(F32)).astype(BF16)


def fold_kernel(keep, arrived, kept, send):
    half = kept.shape[0]
    for i in range(half):
        kept[i] = keep[i].astype(F32) + arrived[i].astype(F32)
        send[i] = (keep[half + i].astype(F32) + arrived[half + i].astype(F32)).astype(BF16)


def fold_last_kernel(keep, arrived, total):
    total[...] = (keep[...].astype(F32) + arrived[...].astype(F32)).astype(BF16)


def concat_kernel(held, arrived, out):
    size = held.shape[0]
    out[0:size] = held[...]
    out[size:] = arrived[...]


def mlp_cut_kernel(pair, arrived, own, *sends, part):
    for c in range(2):
        own[c] = (pair[c].astype(F32) + arrived[1 - c].astype(F32)).astype(BF16)
        for k in (1, 2, 3):
            sends[k - 1][c * part : (c + 1) * part, :] = own[c, (4 + k) * part : (5 + k) * part, :]


def mlp_arrange_kernel(own, near, across, diagonal, held, *, part):
    for c in range(2):
        held[c, : 5 * part] = own[c, : 5 * part, :]
        for k, item in ((1, near), (2, across), (3, diagonal)):
            held[c, (4 + k) * part : (5 + k) * part] = item[c * part : (c + 1) * part, :]


def attention_cut_kernel(pair, arrived, own, *sends, part):
    for c in range(2):
        own[c] = (pair[c].astype(F32) + arrived[1 - c].astype(F32)).astype(BF16)
    lines = jnp.concatenate(
        [own[c, 16 * part :, :].astype(F32)[0:4] for c in range(2)] + [jnp.zeros((LINES - 8, 128), F32)], axis=0
    ).astype(BF16)
    for k in (1, 2, 3):
        for c in range(2):
            sends[k - 1][c * 3 * part : (c + 1) * 3 * part, :] = own[c, 4 * k * part : (4 * k + 3) * part, :]
        sends[k - 1][6 * part :, :] = lines


def attention_arrange_kernel(own, near, across, diagonal, held, *, part):
    for c in range(2):
        lines = [own[c, 16 * part :, :].astype(F32)[0:4]]
        held[c, 0 : 3 * part] = own[c, 0 : 3 * part, :]
        for k, item in ((1, near), (2, across), (3, diagonal)):
            held[c, 4 * k * part : (4 * k + 3) * part] = item[c * 3 * part : (c + 1) * 3 * part, :]
            lines.append(item[6 * part :, :].astype(F32)[4 * c : 4 * c + 4])
        for k in range(4):
            held[c, (4 * k + 3) * part : (4 * k + 4) * part] = own[c, (4 * k + 3) * part : (4 * k + 4) * part, :]
        held[c, 16 * part :] = jnp.concatenate(lines, axis=0).astype(BF16)


def finish_kernel(keep, arrived, tok, cot, out, grad):
    for slot in range(2):
        tokens = tok[slot].astype(F32)
        out[slot] = (tokens + keep[slot, 0] + arrived[slot, 0].astype(F32)).astype(BF16)
        e = keep[slot, 1] + arrived[slot, 1].astype(F32)
        hat, root = normalized(tokens)
        mean_e = jnp.mean(e, axis=-1, keepdims=True)
        mean_eh = jnp.mean(e * hat, axis=-1, keepdims=True)
        grad[slot] = cot[slot * 128 : (slot + 1) * 128, :].astype(F32) + root * (e - mean_e - hat * mean_eh)


def mlp_place_kernel(held, arrived, shrink_out, expand_out, *, split):
    me, mine = lax.axis_index("shard"), lax.axis_index("replica")
    part = 128 // split
    half = split // 2
    for i, c in enumerate(chunk_index(me, split, 0)):
        block = (held if i < half else arrived)[i % half].astype(F32)
        shrink_out[pl.ds(pl.multiple_of((mine ^ c) * 4 * part, 4 * part), 4 * part), :] = block[: 4 * part]
        rows = pl.ds(pl.multiple_of((mine ^ c) * part, part), part)
        for k in range(4):
            columns = pl.ds(pl.multiple_of((me ^ k) * 512, 512), 512)
            expand_out[rows, columns] = block[(4 + k) * part : (5 + k) * part]


def attention_place_kernel(
    held, arrived, joined_out, dense_out, bias_out, dense_bias_out, expand_bias_out, shrink_bias_out,
    gain1_out, shift1_out, gain2_out, shift2_out, vec_s, bias_s, *, split,
):
    me, mine = lax.axis_index("shard"), lax.axis_index("replica")
    part = 128 // split
    half = split // 2
    for i, c in enumerate(chunk_index(me, split, 0)):
        block = (held if i < half else arrived)[i % half].astype(F32)
        r = mine ^ c
        rows = pl.ds(pl.multiple_of(r * part, part), part)
        for k in range(4):
            tiles = [block[(4 * k + t) * part : (4 * k + t + 1) * part] for t in range(4)]
            for third in range(3):
                columns = pl.ds(pl.multiple_of(third * D + (me ^ k) * 128, 128), 128)
                joined_out[rows, columns] = tiles[third]
            dense_out[rows, k * 128 : (k + 1) * 128] = tiles[3]
        vec_s[r] = block[16 * part :]

    row = lax.broadcasted_iota(jnp.int32, (LINES, 128), 0)
    for line, target in ((0, gain1_out), (1, shift1_out), (2, gain2_out), (3, shift2_out)):
        target[...] = jnp.sum(jnp.where(row % 4 == me, vec_s[line], 0.0), axis=0)
    dense_line = jnp.sum(jnp.where(row == me, vec_s[6], 0.0), axis=0)
    dense_bias_out[...] = dense_line
    shrink_bias_out[...] = dense_line
    for k in range(4):
        for third in range(3):
            columns = pl.ds(pl.multiple_of(third * D + (me ^ k) * 128, 128), 128)
            bias_s[0:1, columns] = vec_s[4, 4 * k + third : 4 * k + third + 1]
    bias_out[...] = bias_s[0:1, pl.ds(pl.multiple_of(me * 384, 128), 384)].reshape(384)
    expand_bias_out[...] = jnp.concatenate([vec_s[5, q : q + 1] for q in range(4)], axis=1).reshape(512)


def rope_table(length):
    half = ROT // 2
    freqs = (10000.0 ** (-2.0 * np.arange(half, dtype=np.float64) / ROT)).astype(np.float32)
    angles = np.arange(length, dtype=np.float32)[:, None] * freqs[None, :]
    cosine = np.ones((length, HEAD_DIM), np.float32)
    up = np.zeros((length, HEAD_DIM), np.float32)
    down = np.zeros((length, HEAD_DIM), np.float32)
    cosine[:, :half] = np.cos(angles)
    cosine[:, half:ROT] = np.cos(angles)
    up[:, :half] = -np.sin(angles)
    down[:, half:ROT] = np.sin(angles)
    return np.concatenate([np.tile(part, (1, 2)) for part in (cosine, up, down)], axis=1)


def per_device(
    tokens,
    cotangent,
    segments,
    pad_mask,
    slot_table,
    joined_weight,
    joined_bias,
    dense_weight,
    dense_bias,
    expand_weight,
    expand_bias,
    shrink_weight,
    shrink_bias,
    first_gain,
    first_shift,
    second_gain,
    second_shift,
):
    replicas = lax.axis_size("replica")
    me = lax.axis_index("shard")
    mine = lax.axis_index("replica")
    part = 128 // replicas
    split = replicas if part % 16 == 0 and replicas >= 8 else 0
    steps = replicas.bit_length() - 1
    smem = pl.BlockSpec(memory_space=pltpu.SMEM)
    vmem = pl.BlockSpec(memory_space=pltpu.VMEM)
    shaped = jax.ShapeDtypeStruct

    def call(kernel, name, *, work, outs, scratch, args, limit=12):
        return pl.pallas_call(
            kernel,
            cost_estimate=pl.CostEstimate(flops=work, bytes_accessed=work // 300, transcendentals=0),
            out_shape=tuple(outs),
            in_specs=[vmem] * len(args),
            out_specs=(vmem,) * len(outs),
            scratch_shapes=[pltpu.VMEM(*item) for item in scratch],
            compiler_params=pltpu.CompilerParams(vmem_limit_bytes=limit * 1024 * 1024),
            name=name,
        )(*args)

    small = functools.partial(call, work=1000, scratch=[], limit=8)

    tok = tokens[0].reshape(256, D)
    tok_across = exchange(tok, "shard", 2)
    tok_near = exchange(tok, "shard", 1)
    half_block, joined_block = shaped((64, D), BF16), shaped((128, 384), BF16)
    dy, near_send, expand_y, expand_d, joined_y, joined_d = pl.pallas_call(
        pack_kernel,
        cost_estimate=pl.CostEstimate(flops=2 * 10**9, bytes_accessed=6 * 10**6, transcendentals=0),
        out_shape=(
            shaped((256 + META, D), BF16), shaped((2, 128, D), BF16), half_block, half_block, joined_block, joined_block
        ),
        in_specs=[smem] + [pl.BlockSpec(memory_space=pltpu.HBM)] * len(PACKED),
        out_specs=(vmem,) * 6,
        scratch_shapes=[pltpu.VMEM(*item) for item in PACKED] + [pltpu.SemaphoreType.DMA((len(PACKED),))],
        compiler_params=pltpu.CompilerParams(vmem_limit_bytes=60 * 1024 * 1024),
        name="pack_weights",
    )(
        slot_table, joined_weight, expand_weight, cotangent[0], segments[0], pad_mask[0], joined_bias,
        first_gain, first_shift, second_gain, second_shift,
    )
    near = exchange(near_send, "shard", 1)
    expand_y = exchange(expand_y, "shard", 2)
    expand_d = exchange(expand_d, "shard", 3)
    dy_near = exchange(dy, "shard", 1)
    dy_across = exchange(tied(dy, expand_y, expand_d, tok_across), "shard", 2)
    tok_far = exchange(tok_across, "shard", 1)
    (dy_own,) = small(copy_kernel, "hold_rows", outs=[shaped(dy.shape, BF16)], args=(dy,))
    expand_x = exchange(tied(jnp.stack([expand_y, expand_d]), dy_own, tok_across), "replica", 1)
    held = tied((dy_across, joined_y, joined_d, expand_x, near, dy_near, tok_near, tok_far))
    dy_across, joined_y, joined_d, expand_x, near, dy_near, tok_near, tok_far = held
    joined_y = exchange(joined_y, "shard", 2)
    joined_d = exchange(joined_d, "shard", 3)
    dy_far = exchange(dy_across, "shard", 1)
    toks = (tok, tok_near, tok_across, tok_far)
    dys = (dy_own, dy_near, dy_across, dy_far)

    xor4 = me ^ jnp.arange(4, dtype=jnp.int32)
    order = jnp.where(me % 2 == 0, *[jnp.asarray(xor_order(stages_of(replicas, core)), jnp.int32) for core in (0, 1)])

    def halves(chunks):
        ordered = chunks[mine ^ order]
        return [ordered[: replicas // 2], ordered[replicas // 2 :]]

    def by_owner(pair):
        place_of = jnp.zeros((replicas,), jnp.int32).at[mine ^ order].set(jnp.arange(replicas, dtype=jnp.int32))
        return jnp.concatenate(pair, axis=0)[place_of].astype(F32)

    rows1024 = shaped((1024, 512), BF16)
    vec_shape = shaped((8, D), F32)
    act, inner, expand_all, vec_mlp, meta_all, *mlp_state = call(
        functools.partial(mlp_kernel, split=split),
        "mlp_branch",
        work=4 * 10**9,
        outs=[rows1024, rows1024, shaped((512, 512), BF16), vec_shape, shaped((4, META, D), F32)]
        + ([shaped((replicas // 2, 8 * part, D), BF16)] * 2 if split else [shaped((2, 512, D), BF16)]),
        scratch=[
            ((1024, D), BF16),
            ((1024, D), BF16),
            ((8, 8, 16, D), BF16),
        ],
        args=(*toks, *dys, expand_weight, near, expand_y, expand_d, expand_x, shrink_weight, expand_bias.astype(F32).reshape(1, 512)),
    )
    if not split:
        blocks = mlp_state[0][1].reshape(4, replicas, part, D).transpose(1, 0, 2, 3)[:, xor4]
        mlp_state = halves(
            jnp.concatenate(
                [mlp_state[0][0].reshape(replicas, 4 * part, D), blocks.reshape(replicas, 4 * part, D)], axis=1
            )
        )
    def folded(keep, arrived, last=False, work=1000):
        chunks = keep.shape
        half = shaped((chunks[0] // 2, *chunks[1:]), F32), shaped((chunks[0] // 2, *chunks[1:]), BF16)
        if split and last:
            outs = [shaped(chunks, BF16)]
            return call(fold_last_kernel, "fold", work=work, outs=outs, scratch=[], args=(keep, arrived), limit=8)[0]
        if split:
            return small(fold_kernel, "fold", outs=half, args=(keep, arrived))
        total = keep.astype(F32) + arrived.astype(F32)
        if last:
            return total.astype(BF16)
        return total[: chunks[0] // 2], total[chunks[0] // 2 :].astype(BF16)

    def middle(pair):
        return replica_exchange(pair, steps - 1)

    def doubled(held, arrived, work=1000):
        if split:
            whole = shaped((2 * held.shape[0], *held.shape[1:]), BF16)
            return call(concat_kernel, "double", work=work, outs=[whole], scratch=[], args=(held, arrived), limit=8)[0]
        return jnp.concatenate([held, arrived], axis=0)

    def to_owners(sends):
        return [exchange(send, "shard", k) for k, send in zip((1, 2, 3), sends, strict=True)]

    mlp_state = folded(mlp_state[0], replica_exchange(mlp_state[1], 0))

    half_rows = shaped((2, 2, 128, D), BF16)
    rows_low, rows_full = shaped((512, D), BF16), shaped((512, D), F32)
    common = (
        meta_all, dense_weight,
        dense_bias.astype(F32).reshape(1, 128), shrink_bias.astype(F32).reshape(1, 128), rope_table(4 * 128),
    )
    keep0, send0, joined_part, dense_part, vec_part, joined_all, *second_slot = call(
        functools.partial(attention_kernel, slot=0, split=split),
        "attention_first_slot",
        work=6 * 10**9,
        outs=[half_rows, half_rows, shaped((512, 384), F32), shaped((128, D), F32), vec_shape, shaped((512, 384), BF16)]
        + [rows_full, rows_low, rows_low, rows_low, rows_full, rows_full],
        scratch=[((8, 3 * D), F32)] + [((512, D), BF16)] * 4 + [((4, 2, 128, D), BF16)],
        args=(
            *common, vec_mlp, *toks, *dys, act, inner, expand_all, shrink_weight, joined_weight, near, joined_y, joined_d
        ),
    )
    keep1, send1, *att_state = call(
        functools.partial(attention_kernel, slot=1, split=split),
        "attention_second_slot",
        work=6 * 10**9,
        outs=[half_rows, half_rows]
        + ([shaped((replicas // 2, 16 * part + LINES, 128), BF16)] * 2 if split else [shaped((4, 128, D), BF16), vec_shape]),
        scratch=[((4, 2, 128, D), BF16), ((8, 17, 16, 128), BF16)],
        args=(*common, tied(vec_part, mlp_state[1]), joined_part, dense_part, joined_all, *second_slot),
    )
    if not split:
        blocks = att_state[0].reshape(4, replicas, part, 4, 128).transpose(1, 0, 3, 2, 4)
        blocks = jnp.concatenate([blocks[:, xor4][:, :, :3], blocks[:, :, 3:]], axis=2).reshape(replicas, 16 * part, 128)
        line = jnp.pad(att_state[1].reshape(8, 4, 128), ((0, replicas - 8), (0, LINES - 4), (0, 0))).astype(BF16)
        att_state = halves(jnp.concatenate([blocks, line], axis=1))

    for stage in range(1, steps - 1):
        mlp_state = folded(mlp_state[0], replica_exchange(mlp_state[1], stage), stage == steps - 2)

    mlp_pair = mlp_state
    att_state = folded(att_state[0], replica_exchange(att_state[1], 0))
    from_near = [exchange(tied(send, att_state), "shard", 1) for send in (send0, send1)]
    rows_own, rows_send = small(
        rows_kernel,
        "rows_between_cores",
        outs=[shaped((2, 2, 128, D), F32), shaped((2, 2, 128, D), BF16)],
        args=(keep0, keep1, *from_near),
    )
    rows_arrived = exchange(rows_send, "shard", 2)

    arrived, mlp_new = tied((replica_exchange(att_state[1], 1), middle(mlp_pair)))
    att_pair = folded(att_state[0], arrived, steps == 3, 2 * 10**10)
    for stage in range(2, steps - 1):
        att_pair = folded(att_pair[0], replica_exchange(att_pair[1], stage), stage == steps - 2)
    if split:
        mlp_own, *mlp_sends = small(
            functools.partial(mlp_cut_kernel, part=part),
            "cut_mlp_grads",
            outs=[shaped((2, 8 * part, D), BF16)] + [shaped((2 * part, D), BF16)] * 3,
            args=(mlp_pair, mlp_new),
        )
    else:
        mlp_own = (mlp_pair.astype(F32) + mlp_new[::-1].astype(F32)).astype(BF16)
        mlp_sends = [mlp_own[:, (4 + k) * part : (5 + k) * part].reshape(2 * part, D) for k in (1, 2, 3)]
    att_new, moved = tied((middle(att_pair), to_owners(mlp_sends)))
    if split:
        (mlp_held,) = small(
            functools.partial(mlp_arrange_kernel, part=part),
            "arrange_mlp_grads",
            outs=[shaped((2, 8 * part, D), BF16)],
            args=(mlp_own, *moved),
        )
    else:
        mlp_held = jnp.concatenate([mlp_own[:, : 5 * part], *[item.reshape(2, part, D) for item in moved]], axis=1)

    if split:
        att_own, *att_sends = small(
            functools.partial(attention_cut_kernel, part=part),
            "cut_attention_grads",
            outs=[shaped((2, 16 * part + LINES, 128), BF16)] + [shaped((6 * part + LINES, 128), BF16)] * 3,
            args=(att_pair, att_new),
        )
    else:
        att_own = (att_pair.astype(F32) + att_new[::-1].astype(F32)).astype(BF16)
        lines = att_own[:, 16 * part : 16 * part + 4].reshape(8, 128)
        att_sends = [
            jnp.concatenate([att_own[:, 4 * k * part : (4 * k + 3) * part].reshape(6 * part, 128), lines], axis=0)
            for k in (1, 2, 3)
        ]
    moved = to_owners(att_sends)
    if split:
        (att_held,) = call(
            functools.partial(attention_arrange_kernel, part=part),
            "arrange_attention_grads",
            work=2 * 10**10,
            scratch=[],
            outs=[shaped((2, 16 * part + LINES, 128), BF16)],
            args=(att_own, *moved),
        )
    else:
        pieces, lines = [att_own[:, : 4 * part]], [att_own[:, 16 * part : 16 * part + 4]]
        for k, item in zip((1, 2, 3), moved):
            pieces += [item[: 6 * part].reshape(2, 3 * part, 128), att_own[:, (4 * k + 3) * part : (4 * k + 4) * part]]
            lines.append(item[6 * part :].reshape(2, 4, 128))
        att_held = jnp.concatenate([*pieces, *lines], axis=1)

    for stage in reversed(range(1, steps - 1)):
        mlp_held = doubled(mlp_held, tied(replica_exchange(mlp_held, stage), att_held))
        att_held = doubled(att_held, replica_exchange(att_held, stage), 2 * 10**10)
    mlp_done = mlp_held, replica_exchange(mlp_held, 0)
    att_done = att_held, replica_exchange(att_held, 0)

    def finish(rows_new):
        return small(
            finish_kernel,
            "finish_rows",
            outs=[shaped((2, 128, D), BF16), shaped((2, 128, D), F32)],
            args=(rows_own, rows_new, tokens[0], dy_own),
        )

    if split:
        grad_shrink, grad_expand = small(
            functools.partial(mlp_place_kernel, split=split),
            "place_mlp_grads",
            outs=[shaped((512, D), F32), shaped((128, FF), F32)],
            args=mlp_done,
        )
        output, input_grad = finish(tied(rows_arrived, grad_shrink))
        widths = [384, 128, 512, 128, 128, 128, 128, 128]
        grad_joined, grad_dense, *vectors = call(
            functools.partial(attention_place_kernel, split=split),
            "place_attention_grads",
            work=1000,
            outs=[shaped((128, 3 * D), F32), shaped((128, D), F32)] + [shaped((width,), F32) for width in widths],
            scratch=[((8, LINES, 128), F32), ((8, 3 * D), F32)],
            args=(att_done[0], tied(att_done[1], grad_shrink, output)),
            limit=8,
        )
    else:
        output, input_grad = finish(rows_arrived)
        mlp_all, att_all = by_owner(mlp_done), by_owner(att_done)
        grad_shrink = mlp_all[:, : 4 * part].reshape(512, D)
        blocks = mlp_all[:, 4 * part :].reshape(replicas, 4, part, D)[:, xor4]
        grad_expand = blocks.transpose(0, 2, 1, 3).reshape(128, FF)
        blocks = att_all[:, : 16 * part].reshape(replicas, 4, 4, part, 128)
        grad_dense = blocks[:, :, 3].transpose(0, 2, 1, 3).reshape(128, D)
        grad_joined = blocks[:, xor4, :3].transpose(0, 3, 2, 1, 4).reshape(128, 3 * D)
        lines = att_all[:8, 16 * part :].reshape(8, 4, D)[:, xor4]
        summed = lax.dynamic_slice_in_dim(lines[:4].sum(axis=1), me * 128, 128, axis=1)
        bias_line = lines[4, :, :384].reshape(4, 3, 128).transpose(1, 0, 2).reshape(3 * D)
        dense_line = lax.dynamic_slice_in_dim(lines[6, me], me * 128, 128, axis=0)
        vectors = [
            lax.dynamic_slice_in_dim(bias_line, me * 384, 384, axis=0),
            dense_line,
            lines[5, me],
            dense_line,
            summed[0],
            summed[1],
            summed[2],
            summed[3],
        ]
    return (
        output[None],
        input_grad[None],
        grad_joined,
        vectors[0],
        grad_dense,
        vectors[1],
        grad_expand,
        vectors[2],
        grad_shrink,
        *vectors[3:],
    )


def solution(mesh):
    rows = P("replica", None, "shard", None)
    codes = P("replica", None, "shard")
    matrix = P("shard", None)
    vector = P("shard")
    return jax.shard_map(
        per_device,
        mesh=mesh,
        in_specs=(rows, rows, codes, codes, P("replica", None))
        + (matrix, vector) * 4
        + (vector,) * 4,
        out_specs=(rows, rows) + (matrix, vector) * 4 + (vector,) * 4,
        check_vma=False,
    )
```
